32 devices in a mesh: prefix: 8 (over z, core), branch: 4 (over y, x).
Axes of the slice: x: 2, y: 2, z: 4, core: 2. Of those that a mesh axis runs over, the one named last changes fastest.
Arguments:
- hidden: bfloat16 [3, 32, 8192], P(None, 'branch', 'prefix'), may hold values from -4 to 4
- attn_gain: float32 [8192], P('prefix'), may hold values from 0.1 to 1.9
- ffn_gain: float32 [8192], P('prefix'), may hold values from 0.1 to 1.9
- w_qkv: bfloat16 [8192, 10240], P('prefix', 'branch'), may hold values from -0.0625 to 0.0625
- w_out: bfloat16 [8192, 8192], P('branch', 'prefix'), may hold values from -0.0625 to 0.0625
- w_gate_up: bfloat16 [2, 8192, 28672], P(None, 'prefix', 'branch'), may hold values from -0.0625 to 0.0625
- w_down: bfloat16 [28672, 8192], P('branch', 'prefix'), may hold values from -0.03125 to 0.03125
- tree_kv: bfloat16 [8, 2, 512, 1024], P('prefix'), may hold values from -64 to 64
- suffix_kv: bfloat16 [32, 2, 512, 1024], P('branch', None, 'prefix'), may hold values from -64 to 64
- parent: int32 [8], replicated, may hold values from -1 to 6, as said below
- block_map: int32 [8], replicated, may hold values from 0 to 7, each once
- leaf: int32 [32], P('branch'), may hold values from 0 to 7
- suffix_len: int32 [32], P('branch'), may hold values from 1 to 512, as said below
Outputs:
- out: bfloat16 [3, 32, 8192], P(None, 'branch', 'prefix')
- new_kv: bfloat16 [32, 2, 3, 1024], P('branch')
The draws below stay inside these ranges and needn't reach their ends.
Inputs may be any that keep to these rules, and one draw needn't show every extreme that they name: Block 0 is the root with parent -1; every other block n has a parent below n; the last block's parent is block 6. `suffix_len`: some branch has exactly 512 used positions and some exactly 1.
All inputs are finite; a program needn't handle non-finite values.
Results may differ from the reference program's by a relative error of at most 0.01225.
The reference program's roundings to bfloat16 on the way count: a program that leaves them out, or rounds other values in their place, can miss the bound.
Values may be sent and summed in bfloat16 or wider, within the bound.
No kernel may reach another device: no remote copies, remote signals or barrier semaphores. Data moves between devices by JAX's collectives and lax.ppermute only.
A program may use at most 128 MiB of HBM per device.

```python
import jax
import jax.numpy as jnp
from jax import lax

D = 8192
HEADS = 64
KVH = 8
HD = 128
FF = 28672
BLK = 512
STEPS = 3
QKV = 10240
NBLK = 8
ROWS = 32
SUF = 512


def strong_keys(key, array_shape, base, share, low, high):
    first_key, second_key, third_key = jax.random.split(key, 3)
    keyside = jnp.array([1.0, 0.0], dtype=jnp.float32).reshape(1, 2, 1, 1)
    token_shape = array_shape[:-1] + (1,)
    chosen = jax.random.uniform(first_key, token_shape, jnp.float32) < share
    magnitude = jax.random.uniform(second_key, array_shape, jnp.float32, low, high)
    signs = jnp.where(jax.random.uniform(third_key, array_shape, jnp.float32) < 0.5, -1.0, 1.0)
    strong = signs * magnitude
    return jnp.where(chosen & (keyside > 0.5), strong, base)


def bounded_entries(key, array_shape):
    first_key, second_key = jax.random.split(key)
    component = jnp.array([1.0, 2.0], dtype=jnp.float32).reshape(1, 2, 1, 1)
    base = jax.random.truncated_normal(first_key, -4.0, 4.0, array_shape, jnp.float32) * component
    return strong_keys(second_key, array_shape, base, 0.08, 64.0, 64.0)


def draw_tree_kv(key, part):
    key = jax.random.fold_in(key, 3)
    array_shape = (NBLK, 2, BLK, KVH * HD)
    return bounded_entries(key, array_shape).astype(jnp.bfloat16)


def draw_suffix_kv(key, part):
    key = jax.random.fold_in(key, 4)
    array_shape = (ROWS, 2, SUF, KVH * HD)
    return bounded_entries(key, array_shape).astype(jnp.bfloat16)


def draw_parent(key, part):
    key = jax.random.fold_in(key, 5)
    node_ids = jnp.arange(NBLK, dtype=jnp.int32)
    picked = jax.random.randint(key, (NBLK,), 0, NBLK)
    chosen = jnp.where(node_ids > 0, picked % jnp.maximum(node_ids, 1), -1)
    chosen = jnp.where(node_ids == NBLK - 1, NBLK - 2, chosen)
    return chosen.astype(jnp.int32)


def draw_suffix_len(key, part):
    key = jax.random.fold_in(key, 7)
    first_key, second_key = jax.random.split(key)
    lengths = jax.random.randint(first_key, (ROWS,), 1, SUF + 1)
    chosen_rows = jax.random.permutation(second_key, ROWS)
    return lengths.at[chosen_rows[0]].set(SUF).at[chosen_rows[1]].set(1).astype(jnp.int32)


def with_ends(values, own_key, low, high):
    extent = values.shape
    index_at = [jax.random.randint(jax.random.fold_in(own_key, axis), (), 0, extent[axis]) for axis in range(len(extent))]
    values = values.at[tuple(index_at)].set(low)
    longest = extent.index(max(extent))
    index_at[longest] = (index_at[longest] + 1) % extent[longest]
    return values.at[tuple(index_at)].set(high)


def shard_levels(own_key, dims, shards, low, high):
    def one(axis_at, blocks):
        steps = jax.random.uniform(jax.random.fold_in(jax.random.fold_in(own_key, 6), axis_at), (blocks,), jnp.float32, low / len(shards), high / len(shards))
        return jnp.repeat(jnp.exp(steps), dims[axis_at] // blocks).reshape((-1,) + (1,) * (len(dims) - axis_at - 1))

    level = one(*shards[0])
    for cut in shards[1:]:
        level = level * one(*cut)
    return level


def centred(stream_key, extent, spread, most, cuts=(), kind=jnp.bfloat16):
    drawn = spread * jax.random.normal(stream_key, extent, jnp.float32)
    if cuts:
        drawn = drawn * shard_levels(stream_key, extent, cuts, -0.22, 0.18)
    return jnp.clip(drawn, -most, most).astype(kind)


def setup_inputs(seed: int = 0) -> dict:
    splits = jax.random.split(jax.random.key(seed), 14)
    return {
        "hidden": centred(splits[0], (STEPS, ROWS, D), 0.5, 4.0, ((1, 4), (2, 8))),
        "attn_gain": jnp.clip(1.0 + 0.18 * jax.random.normal(splits[1], (D,), jnp.float32), 0.1, 1.9),
        "ffn_gain": jnp.clip(1.0 + 0.18 * jax.random.normal(splits[2], (D,), jnp.float32), 0.1, 1.9),
        "w_qkv": centred(splits[3], (D, QKV), D ** -0.5, 0.0625, ((0, 8), (1, 4))),
        "w_out": centred(splits[4], (HEADS * HD, D), (HEADS * HD) ** -0.5, 0.0625, ((0, 4), (1, 8))),
        "w_gate_up": centred(splits[5], (2, D, FF), D ** -0.5, 0.0625, ((1, 8), (2, 4))),
        "w_down": centred(splits[6], (FF, D), FF ** -0.5, 0.03125, ((0, 4), (1, 8))),
        "tree_kv": draw_tree_kv(jax.random.fold_in(splits[13], 71), 0),
        "suffix_kv": draw_suffix_kv(jax.random.fold_in(splits[13], 71), 0),
        "parent": draw_parent(jax.random.fold_in(splits[13], 71), 0),
        "block_map": jax.random.permutation(splits[10], NBLK).astype(jnp.int32),
        "leaf": with_ends(jax.random.randint(splits[11], (ROWS,), 0, NBLK), jax.random.fold_in(splits[11], 1), 0, NBLK - 1).astype(jnp.int32),
        "suffix_len": draw_suffix_len(jax.random.fold_in(splits[13], 71), 0),
    }


EPS = 1e-05
ROPE_BASE = 500000.0
FLOOR = -1e+30

def rotate(values, position):
    half_dim = values.shape[-1] // 2
    frequency = ROPE_BASE ** (-(jnp.arange(half_dim, dtype=jnp.float32) * 2.0 / values.shape[-1]))
    angles = position.astype(jnp.float32)[..., None] * frequency
    cosine = jnp.cos(angles)
    sine_part = jnp.sin(angles)
    first_half = values[..., :half_dim]
    second_half = values[..., half_dim:]
    return jnp.concatenate([first_half * cosine - second_half * sine_part, second_half * cosine + first_half * sine_part], axis=-1)

def path_members(leaf, parent):
    node_ids = jnp.arange(parent.shape[0], dtype=jnp.int32)

    def climb_step(index, carry):
        current, member = carry
        hits = node_ids[None, :] == current[:, None]
        member = jnp.maximum(member, hits.astype(jnp.int32))
        upward = lax.optimization_barrier(jnp.sum(jnp.where(hits, parent[None, :], 0), axis=1))
        current = jnp.where(current >= 0, upward, -1).astype(jnp.int32)
        return (current, member)
    start = (leaf.astype(jnp.int32), jnp.zeros((leaf.shape[0], parent.shape[0]), jnp.int32))
    return lax.fori_loop(0, parent.shape[0], climb_step, start)[1]

def reference(hidden, attn_gain, ffn_gain, w_qkv, w_out, w_gate_up, w_down, tree_kv, suffix_kv, parent, block_map, leaf, suffix_len):
    step_count, row_count, width = hidden.shape
    hid_float = hidden.astype(jnp.float32)
    normed = (hid_float * lax.rsqrt(lax.optimization_barrier(jnp.mean(hid_float * hid_float, axis=2, keepdims=True)) + EPS) * attn_gain).astype(jnp.bfloat16)
    projected = jnp.dot(normed.reshape(step_count * row_count, width), w_qkv, preferred_element_type=jnp.float32)
    projected = projected.astype(jnp.bfloat16).reshape(step_count, row_count, -1)
    q_width = HEADS * HD
    kv_width = KVH * HD
    queries = projected[..., :q_width].reshape(step_count, row_count, KVH, HEADS // KVH, HD).astype(jnp.float32)
    new_keys = projected[..., q_width:q_width + kv_width].reshape(step_count, row_count, KVH, HD).astype(jnp.float32)
    new_values = projected[..., q_width + kv_width:].reshape(step_count, row_count, KVH, HD)
    member = path_members(leaf, parent)
    path_depth = lax.optimization_barrier(jnp.sum(member, axis=1))
    position = BLK * path_depth[None, :] + suffix_len[None, :] + jnp.arange(step_count, dtype=jnp.int32)[:, None]
    query_rot = rotate(queries, position[:, :, None, None]).astype(jnp.bfloat16)
    key_rot = rotate(new_keys, position[:, :, None]).astype(jnp.bfloat16)
    new_kv = jnp.stack([key_rot.reshape(step_count, row_count, kv_width), new_values.reshape(step_count, row_count, kv_width)], axis=0).transpose(2, 0, 1, 3)
    owned_slots = (block_map[:, None] == jnp.arange(NBLK, dtype=jnp.int32)[None, :]).astype(jnp.int32)
    slot_member = lax.optimization_barrier(jnp.max(member[:, :, None] * owned_slots[None, :, :], axis=1)) > 0
    tree_allowed = jnp.repeat(slot_member, BLK, axis=1)
    tree_keys = tree_kv[:, 0].reshape(NBLK * BLK, KVH, HD).astype(jnp.float32)
    tree_values = tree_kv[:, 1].reshape(NBLK * BLK, KVH, HD).astype(jnp.float32)
    score_scale = HD ** (-0.5)
    causal = jnp.arange(step_count)[None, :] <= jnp.arange(step_count)[:, None]
    suffix_ids = jnp.arange(SUF, dtype=jnp.int32)

    def one_row(row_items):
        q_row, k_row, v_row, suffix_row, tree_row, length = row_items
        suffix_keys = suffix_row[0].reshape(SUF, KVH, HD).astype(jnp.float32)
        suffix_values = suffix_row[1].reshape(SUF, KVH, HD).astype(jnp.float32)
        all_keys = jnp.concatenate([tree_keys, suffix_keys, k_row.astype(jnp.float32)], axis=0)
        all_values = jnp.concatenate([tree_values, suffix_values, v_row.astype(jnp.float32)], axis=0)
        scores = jnp.einsum('skgh,nkh->skgn', q_row.astype(jnp.float32), all_keys) * score_scale
        allowed = jnp.concatenate([jnp.broadcast_to(tree_row[None, :], (step_count, tree_row.shape[0])), jnp.broadcast_to((suffix_ids < length)[None, :], (step_count, SUF)), causal], axis=1)[:, None, None, :]
        masked = jnp.where(allowed, scores, FLOOR)
        highest = lax.optimization_barrier(jnp.max(masked, axis=-1, keepdims=True))
        weights = jnp.where(allowed, jnp.exp(masked - highest), 0.0)
        result = jnp.einsum('skgn,nkh->skgh', weights, all_values) / lax.optimization_barrier(jnp.sum(weights, axis=-1))[..., None]
        return result.reshape(step_count, q_width)
    attended = lax.map(one_row, (query_rot.transpose(1, 0, 2, 3, 4), key_rot.transpose(1, 0, 2, 3), new_values.transpose(1, 0, 2, 3), suffix_kv, tree_allowed, suffix_len))
    attended = attended.transpose(1, 0, 2).astype(jnp.bfloat16)
    mixed_out = jnp.dot(attended.reshape(step_count * row_count, q_width), w_out, preferred_element_type=jnp.float32)
    residual = (hid_float.reshape(step_count * row_count, width) + mixed_out).astype(jnp.bfloat16)
    res_float = residual.astype(jnp.float32)
    normed2 = (res_float * lax.rsqrt(lax.optimization_barrier(jnp.mean(res_float * res_float, axis=1, keepdims=True)) + EPS) * ffn_gain).astype(jnp.bfloat16)
    gate = jnp.dot(normed2, w_gate_up[0], preferred_element_type=jnp.float32)
    up_part = jnp.dot(normed2, w_gate_up[1], preferred_element_type=jnp.float32)
    activation = (jax.nn.silu(gate) * up_part).astype(jnp.bfloat16)
    result_rows = res_float + jnp.dot(activation, w_down, preferred_element_type=jnp.float32)
    return (result_rows.astype(jnp.bfloat16).reshape(step_count, row_count, width), new_kv)
```

```python
import functools

import jax
import jax.numpy as jnp
from jax import lax
from jax.experimental import pallas as pl
from jax.experimental.pallas import tpu as pltpu
from jax.sharding import Mesh
from jax.sharding import PartitionSpec as P

HEADS = 64
KVH = 8
HD = 128
GROUP = HEADS // KVH
BLK = 512
CORES = 2
SUB = 8
LANE = 128

EPS = 1e-05
ROPE_BASE = 500000.0
FLOOR = -1e30
LOWEST = -1e29
F32 = jnp.float32
BF16 = jnp.bfloat16
EVERY = ("z", "core", "branch")


def ceil_div(a, b):
    return -(-a // b)


def whole(shape):
    return pl.BlockSpec(shape, lambda *_: (0,) * len(shape))


def params(mib):
    return pltpu.CompilerParams(vmem_limit_bytes=mib * 2**20)


def swap(x, axis, n, k):
    return lax.ppermute(x, axis, [(i, i ^ k) for i in range(n)])


def exchange(x, axes):
    return lax.all_to_all(x, axes, split_axis=0, concat_axis=0, tiled=True)


def spread(x, axes):
    n = lax.axis_size(axes)
    return exchange(jnp.broadcast_to(x[None], (n,) + x.shape), axes)


def stat_tile(rows):
    lane = lax.broadcasted_iota(jnp.int32, (SUB, LANE), 1)
    tile = jnp.zeros((SUB, LANE), F32)
    for s, x in enumerate(rows):
        tile = jnp.where(lane == s, jnp.sum(x * x, axis=1, keepdims=True), tile)
    return tile


def stats_kernel(hidden, stats):
    tile = stat_tile([hidden[s].astype(F32) for s in range(hidden.shape[0])])
    stats[...] = jnp.broadcast_to(tile[None], stats.shape)


def residual_kernel(hidden, parts, residual, stats):
    steps = hidden.shape[0]
    rows = []
    for s in range(steps):
        total = hidden[s].astype(F32)
        mixed = parts[0, s].astype(F32)
        for b in range(1, parts.shape[0]):
            mixed = mixed + parts[b, s].astype(F32)
        rounded = (total + mixed).astype(BF16)
        residual[s] = rounded
        rows.append(rounded.astype(F32))
    stats[...] = jnp.broadcast_to(stat_tile(rows)[None], stats.shape)


def normed_rows(parts, stats, gain, branch, width):
    out = []
    for k, part in enumerate(parts):
        b = branch ^ k
        total = stats[0, b]
        for p in range(1, stats.shape[0]):
            total = total + stats[p, b]
        scale = lax.rsqrt(total / width + EPS)
        for s in range(part.shape[0]):
            out.append(part[s].astype(F32) * scale[:, s : s + 1] * gain[...])
    return jnp.concatenate(out, axis=0).astype(BF16)


def qkv_kernel(width, heads_step, tiles, ids, *refs):
    *parts, stats, gain, w, out, lhs = refs
    step = pl.program_id(0)

    @pl.when(step == 0)
    def _():
        lhs[...] = normed_rows(parts, stats, gain, ids[2], width)

    acc = jnp.dot(lhs[...], w[...], preferred_element_type=F32)
    steps = parts[0].shape[0]
    for hh in range(heads_step):
        for s in range(steps):
            index = (step * heads_step + hh) * steps + s
            owner = index // tiles
            at = index % tiles
            side = (owner % CORES) ^ ids[1]
            for k in range(len(parts)):
                row = (k * steps + s) * SUB
                out[side, owner // CORES, ids[2] ^ k, at] = acc[
                    row : row + SUB, hh * HD : (hh + 1) * HD
                ]


def project_qkv(ids, parts, stats, gain, w, width, prefix):
    branches = len(parts)
    steps = parts[0].shape[0]
    depth, columns = w.shape
    heads = columns // HD
    heads_step = max(n for n in range(1, 6) if heads % n == 0)
    tiles = ceil_div(heads * steps, prefix)
    shape = (CORES, prefix // CORES, branches, tiles, SUB, HD)
    return pl.pallas_call(
        functools.partial(qkv_kernel, width, heads_step, tiles),
        grid_spec=pltpu.PrefetchScalarGridSpec(
            num_scalar_prefetch=1,
            grid=(heads // heads_step,),
            in_specs=[whole(p.shape) for p in parts]
            + [
                whole(stats.shape),
                whole(gain.shape),
                pl.BlockSpec((depth, heads_step * HD), lambda i, _: (0, i)),
            ],
            out_specs=whole(shape),
            scratch_shapes=[pltpu.VMEM((branches * steps * SUB, depth), BF16)],
        ),
        out_shape=jax.ShapeDtypeStruct(shape, F32),
        compiler_params=params(40),
        name="qkv",
    )(ids, *parts, stats, gain, w)


def gate_up_kernel(width, ids, *refs):
    *parts, stats, gain, w, out, lhs = refs

    @pl.when(pl.program_id(0) == 0)
    def _():
        lhs[...] = normed_rows(parts, stats, gain, ids[2], width)

    for half in range(2):
        out[0, 0, half] = jnp.dot(lhs[...], w[half], preferred_element_type=F32).astype(BF16)


def project_gate_up(ids, parts, stats, gain, w, width, prefix):
    branches = len(parts)
    rows = branches * parts[0].shape[0] * SUB
    _, depth, columns = w.shape
    unit = ceil_div(columns // LANE, prefix) * LANE
    shape = (CORES, prefix // CORES, 2, rows, unit)
    return pl.pallas_call(
        functools.partial(gate_up_kernel, width),
        grid_spec=pltpu.PrefetchScalarGridSpec(
            num_scalar_prefetch=1,
            grid=(columns // unit,),
            in_specs=[whole(p.shape) for p in parts]
            + [
                whole(stats.shape),
                whole(gain.shape),
                pl.BlockSpec((2, depth, unit), lambda i, _: (0, 0, i)),
            ],
            out_specs=pl.BlockSpec(
                (1, 1, 2, rows, unit),
                lambda i, ids: ((i % CORES) ^ ids[1], i // CORES, 0, 0, 0),
            ),
            scratch_shapes=[pltpu.VMEM((rows, depth), BF16)],
        ),
        out_shape=jax.ShapeDtypeStruct(shape, BF16),
        compiler_params=params(40),
        name="gate_up",
    )(ids, *parts, stats, gain, w)


def mix_kernel(steps, tiles, attended, w, out, lhs):
    branches = attended.shape[1]

    @pl.when(pl.program_id(0) == 0)
    def _():
        for j in range(lhs.shape[1] // HD):
            column = []
            for b in range(branches):
                for s in range(steps):
                    index = j * steps + s
                    column.append(attended[index // tiles, b, index % tiles].astype(F32))
            lhs[:, j * HD : (j + 1) * HD] = jnp.concatenate(column, axis=0).astype(BF16)

    acc = jnp.dot(lhs[...], w[...], preferred_element_type=F32)
    for b in range(branches):
        for s in range(steps):
            row = (b * steps + s) * SUB
            out[b, s] = acc[row : row + SUB].astype(BF16)


def mix_heads(attended, w, steps):
    _, branches, tiles = attended.shape[:3]
    depth, columns = w.shape
    unit = min(columns, 256)
    rows = branches * steps * SUB
    return pl.pallas_call(
        functools.partial(mix_kernel, steps, tiles),
        grid=(columns // unit,),
        in_specs=[whole(attended.shape), pl.BlockSpec((depth, unit), lambda i: (0, i))],
        out_specs=pl.BlockSpec((branches, steps, SUB, unit), lambda i: (0, 0, 0, i)),
        out_shape=jax.ShapeDtypeStruct((branches, steps, SUB, columns), BF16),
        scratch_shapes=[pltpu.VMEM((rows, depth), BF16)],
        compiler_params=params(40),
        name="mix",
    )(attended, w)


def down_kernel(steps, ids, own, other, w, out, acc):
    step = pl.program_id(0)
    mine = (step % CORES) == ids[1]

    @pl.when(step == 0)
    def _():
        acc[...] = jnp.zeros_like(acc)

    @pl.when(mine)
    def _():
        acc[...] += jnp.dot(own[0], w[...], preferred_element_type=F32)

    @pl.when(jnp.logical_not(mine))
    def _():
        acc[...] += jnp.dot(other[0], w[...], preferred_element_type=F32)

    @pl.when(step == pl.num_programs(0) - 1)
    def _():
        for b in range(out.shape[0]):
            for s in range(steps):
                row = ((ids[2] ^ b) * steps + s) * SUB
                out[b, s] = acc[pl.ds(pl.multiple_of(row, SUB), SUB), :].astype(BF16)


def project_down(ids, own, other, w, branches, steps):
    _, rows, unit = own.shape
    columns = w.shape[1]
    piece = pl.BlockSpec((1, rows, unit), lambda i, _: (i // CORES, 0, 0))
    shape = (branches, steps, SUB, columns)
    return pl.pallas_call(
        functools.partial(down_kernel, steps),
        grid_spec=pltpu.PrefetchScalarGridSpec(
            num_scalar_prefetch=1,
            grid=(w.shape[0] // unit,),
            in_specs=[piece, piece, pl.BlockSpec((unit, columns), lambda i, _: (i, 0))],
            out_specs=whole(shape),
            scratch_shapes=[pltpu.VMEM((rows, columns), F32)],
        ),
        out_shape=jax.ShapeDtypeStruct(shape, BF16),
        compiler_params=params(40),
        name="down",
    )(ids, own, other, w)


def prepare_kernel(steps, blocks_here, suffix_here, prefix, ids, parent, block_map, leaf, length, pos, bias):
    rows = leaf.shape[0]
    place = ids[0] * CORES + ids[1]
    sub = lax.broadcasted_iota(jnp.int32, (SUB, LANE), 0)
    base = jnp.zeros((SUB, LANE), jnp.int32)
    used = jnp.zeros((SUB, LANE), jnp.int32)
    owned = [jnp.zeros((SUB, LANE), jnp.int32) for _ in range(blocks_here)]
    for r in range(rows):
        current = leaf[r]
        depth = jnp.int32(0)
        hits = [jnp.int32(0)] * blocks_here
        for _ in range(parent.shape[0]):
            valid = current >= 0
            at = jnp.maximum(current, 0)
            slot = jnp.where(valid, block_map[at], -1)
            hits = [h + (slot == place * blocks_here + n).astype(jnp.int32) for n, h in enumerate(hits)]
            depth = depth + valid.astype(jnp.int32)
            current = jnp.where(valid, parent[at], -1)
        base = jnp.where(sub == r, BLK * depth + length[r], base)
        used = jnp.where(sub == r, length[r], used)
        owned = [jnp.where(sub == r, h, o) for h, o in zip(hits, owned)]
    tree = blocks_here * BLK
    keys = SUB * suffix_here
    sub_keys = lax.broadcasted_iota(jnp.int32, (SUB, keys), 0)
    key = lax.broadcasted_iota(jnp.int32, (SUB, keys), 1)
    suffix_ok = (key // suffix_here == sub_keys) & (
        place * suffix_here + key % suffix_here < used[:, :1]
    )
    suffix = jnp.where(suffix_ok, 0.0, FLOOR)
    lane = lax.broadcasted_iota(jnp.int32, (SUB, LANE), 1)
    for s in range(steps):
        pos[s] = (base + s).astype(F32)
        row = slice(s * SUB, (s + 1) * SUB)
        for n in range(blocks_here):
            bias[row, n * BLK : (n + 1) * BLK] = jnp.broadcast_to(
                jnp.where(owned[n][:, :1] > 0, 0.0, FLOOR), (SUB, BLK)
            )
        bias[row, tree : tree + keys] = suffix
        new_ok = (lane % SUB == sub) & (lane // SUB <= s) & (place == 0)
        bias[row, tree + keys : tree + keys + LANE] = jnp.where(new_ok, 0.0, FLOOR)


def prepare(ids, parent, block_map, leaf, length, steps, blocks_here, suffix_here, prefix):
    columns = blocks_here * BLK + SUB * suffix_here + LANE
    smem = pl.BlockSpec(memory_space=pltpu.SMEM)
    return pl.pallas_call(
        functools.partial(prepare_kernel, steps, blocks_here, suffix_here, prefix),
        in_specs=[smem] * 5,
        out_shape=[
            jax.ShapeDtypeStruct((steps, SUB, LANE), F32),
            jax.ShapeDtypeStruct((steps * SUB, columns), F32),
        ],
        name="prepare",
    )(ids, parent, block_map, leaf, length)


def attend_kernel(heads_in, tiles_in, heads_out, tiles_out, qkv, cosine, sine, bias, tree, suffix, out, new_kv, sums):
    k = pl.program_id(0)
    steps = cosine.shape[0]
    rows = steps * SUB
    lane = lax.broadcasted_iota(jnp.int32, (SUB, LANE), 1)

    @pl.when(k == 0)
    def _():
        sums[...] = jnp.zeros_like(sums)

    def tile(head, s):
        index = (head % heads_in) * steps + s
        return qkv[index // tiles_in, head // heads_in, index % tiles_in].astype(F32)

    def turned(x, s):
        return x * cosine[s] + pltpu.roll(x, HD // 2, 1) * sine[s]

    query = jnp.concatenate(
        [turned(tile(k * GROUP + g, s), s) for g in range(GROUP) for s in range(steps)], axis=0
    ).astype(BF16)
    keys = [turned(tile(HEADS + k, s), s) for s in range(steps)]
    values = [tile(HEADS + KVH + k, s) for s in range(steps)]
    for s in range(steps):
        new_kv[0, s] = keys[s].astype(BF16)
        new_kv[1, s] = values[s].astype(BF16)
    fill = [jnp.zeros((LANE - rows, HD), F32)]
    sources = [
        (tree[:, 0].reshape(-1, HD), tree[:, 1].reshape(-1, HD)),
        (suffix[:, 0].reshape(-1, HD), suffix[:, 1].reshape(-1, HD)),
        (
            jnp.concatenate(keys + fill, axis=0).astype(BF16),
            jnp.concatenate(values + fill, axis=0).astype(BF16),
        ),
    ]
    scores = []
    start = 0
    highest = jnp.full((GROUP, rows, 1), LOWEST, F32)
    for key, _ in sources:
        count = key.shape[0]
        product = lax.dot_general(
            query, key, (((1,), (1,)), ((), ())), preferred_element_type=F32
        ) * (HD**-0.5)
        product = product.reshape(GROUP, rows, count) + bias[:, start : start + count][None]
        highest = jnp.maximum(highest, jnp.max(product, axis=-1, keepdims=True))
        scores.append(product)
        start += count
    total = jnp.zeros((GROUP, rows, 1), F32)
    acc = jnp.zeros((GROUP * rows, HD), F32)
    for product, (_, value) in zip(scores, sources):
        weight = jnp.exp(product - highest)
        total = total + jnp.sum(weight, axis=-1, keepdims=True)
        acc = acc + jnp.dot(
            weight.reshape(GROUP * rows, -1).astype(BF16), value, preferred_element_type=F32
        )
    some = total > 0
    safe = jnp.where(some, total, 1.0)
    result = acc.reshape(GROUP, rows, HD) / safe
    log_sum = jnp.where(some, highest + jnp.log(safe), LOWEST)
    for g in range(GROUP):
        head = k * GROUP + g
        for s in range(steps):
            index = (head % heads_out) * steps + s
            owner, b, at = index // tiles_out, head // heads_out, index % tiles_out
            row = slice(s * SUB, (s + 1) * SUB)
            out[owner, b, at] = result[g, row].astype(BF16)
            sums[owner, b] = jnp.where(lane == at, log_sum[g, row], sums[owner, b])

    @pl.when(k == pl.num_programs(0) - 1)
    def _():
        for p in range(sums.shape[0]):
            for b in range(sums.shape[1]):
                value = sums[p, b]
                high = value.astype(BF16).astype(F32)
                rest = value - high
                middle = rest.astype(BF16).astype(F32)
                low = rest - middle
                packed = jnp.where(
                    lane < 32,
                    high,
                    jnp.where(lane < 64, pltpu.roll(middle, 32, 1), pltpu.roll(low, 64, 1)),
                )
                out[p, b, tiles_out] = packed.astype(BF16)


def attend(qkv, cosine, sine, bias, tree_kv, suffix_kv, heads_in, heads_out, prefix):
    _, branches, tiles_in = qkv.shape[:3]
    steps = cosine.shape[0]
    tiles_out = ceil_div(heads_out * steps, prefix)
    shape = (prefix, branches, tiles_out + 1, SUB, HD)

    def by_head(array):
        block = array.shape[:-1] + (HD,)
        return pl.BlockSpec(block, lambda k: (0,) * (len(block) - 1) + (k,))

    return pl.pallas_call(
        functools.partial(attend_kernel, heads_in, tiles_in, heads_out, tiles_out),
        grid=(KVH,),
        in_specs=[whole(a.shape) for a in (qkv, cosine, sine, bias)]
        + [by_head(tree_kv), by_head(suffix_kv)],
        out_specs=[
            whole(shape),
            pl.BlockSpec((2, steps, SUB, HD), lambda k: (0, 0, 0, k)),
        ],
        out_shape=[
            jax.ShapeDtypeStruct(shape, BF16),
            jax.ShapeDtypeStruct((2, steps, SUB, KVH * HD), BF16),
        ],
        scratch_shapes=[pltpu.VMEM((prefix, branches, SUB, LANE), F32)],
        compiler_params=params(40),
        name="attend",
    )(qkv, cosine, sine, bias, tree_kv, suffix_kv)


def join_kernel(parts, out):
    prefix, branches, count = parts.shape[:3]
    tiles = count - 1
    for b in range(branches):
        logs = []
        for p in range(prefix):
            packed = parts[p, b, tiles].astype(F32)
            logs.append(packed + pltpu.roll(packed, LANE - 32, 1) + pltpu.roll(packed, LANE - 64, 1))
        highest = functools.reduce(jnp.maximum, logs)
        weights = [jnp.exp(x - highest) for x in logs]
        total = functools.reduce(jnp.add, weights)
        weights = [w / total for w in weights]
        for t in range(tiles):
            acc = jnp.zeros((SUB, HD), F32)
            for p in range(prefix):
                acc = acc + parts[p, b, t].astype(F32) * weights[p][:, t : t + 1]
            out[b, t] = acc.astype(BF16)


def join(parts):
    _, branches, count = parts.shape[:3]
    return pl.pallas_call(
        join_kernel,
        out_shape=jax.ShapeDtypeStruct((branches, count - 1, SUB, HD), BF16),
        name="join",
    )(parts)


def body(
    hidden,
    attn_gain,
    ffn_gain,
    w_qkv,
    w_out,
    w_gate_up,
    w_down,
    tree_kv,
    suffix_kv,
    parent,
    block_map,
    leaf,
    suffix_len,
):
    steps, rows, width_dev = hidden.shape
    z_count = lax.axis_size("z")
    branches = lax.axis_size("branch")
    prefix = z_count * CORES
    width = width_dev * prefix
    devices = prefix * branches
    ids = jnp.stack([lax.axis_index("z"), lax.axis_index("core"), lax.axis_index("branch")]).astype(
        jnp.int32
    )

    pos, bias = prepare(
        ids, parent, block_map, leaf, suffix_len, steps, tree_kv.shape[0], suffix_kv.shape[2], prefix
    )
    half = HD // 2
    frequency = ROPE_BASE ** (-(jnp.arange(half, dtype=F32) * 2.0 / HD))
    angles = pos[..., :1] * frequency
    cos, sin = jnp.cos(angles), jnp.sin(angles)
    cosine = jnp.concatenate([cos, cos], axis=-1)
    sine = jnp.concatenate([-sin, sin], axis=-1)

    stats = pl.pallas_call(
        stats_kernel, out_shape=jax.ShapeDtypeStruct((devices, SUB, LANE), F32), name="stats"
    )(hidden)
    stats = exchange(stats, EVERY).reshape(prefix, branches, SUB, LANE)
    parts = [hidden] + [swap(hidden, "branch", branches, k) for k in range(1, branches)]
    part_sums = project_qkv(ids, parts, stats, attn_gain[None], w_qkv, width, prefix)
    chip_sums = part_sums[0] + lax.ppermute(part_sums[1], "core", [(0, 1), (1, 0)])
    tiles = chip_sums.shape[2]
    sent = exchange(chip_sums.reshape(z_count * branches, tiles, SUB, HD), ("z", "branch"))
    summed = jnp.sum(sent.reshape(z_count, branches, tiles, SUB, HD), axis=0).astype(BF16)
    qkv = spread(summed, ("z", "core"))

    heads_in = w_qkv.shape[1] // HD
    heads_out = w_out.shape[0] // HD
    softmax_parts, new_kv = attend(
        qkv, cosine, sine, bias, tree_kv, suffix_kv, heads_in, heads_out, prefix
    )
    new_kv = new_kv.transpose(2, 0, 1, 3)
    tiles_out = softmax_parts.shape[2]
    received = exchange(softmax_parts.reshape(devices, tiles_out, SUB, HD), EVERY)
    attended = join(received.reshape(prefix, branches, tiles_out, SUB, HD))
    attended = spread(attended, ("z", "core"))

    mixed = exchange(mix_heads(attended, w_out, steps), "branch")
    residual, stats = pl.pallas_call(
        residual_kernel,
        out_shape=[
            jax.ShapeDtypeStruct(hidden.shape, BF16),
            jax.ShapeDtypeStruct((devices, SUB, LANE), F32),
        ],
        name="residual",
    )(hidden, mixed)
    stats = exchange(stats, EVERY).reshape(prefix, branches, SUB, LANE)
    parts = [residual] + [swap(residual, "branch", branches, k) for k in range(1, branches)]
    part_sums = project_gate_up(ids, parts, stats, ffn_gain[None], w_gate_up, width, prefix)
    chip_sums = part_sums[0].astype(F32) + lax.ppermute(
        part_sums[1], "core", [(0, 1), (1, 0)]
    ).astype(F32)
    gathered = jnp.sum(exchange(chip_sums.astype(BF16), "z").astype(F32), axis=0)
    activation = (jax.nn.silu(gathered[0]) * gathered[1]).astype(BF16)
    own = spread(activation, "z")
    other = lax.ppermute(own, "core", [(0, 1), (1, 0)])
    down = exchange(project_down(ids, own, other, w_down, branches, steps), "branch")
    result = (residual.astype(F32) + jnp.sum(down.astype(F32), axis=0)).astype(BF16)
    return (result, new_kv)


def solution(mesh):
    prefix, branches = mesh.shape["prefix"], mesh.shape["branch"]
    split = Mesh(mesh.devices.reshape(prefix // CORES, CORES, branches), EVERY)
    along = ("z", "core")
    placed = (
        P(None, "branch", along),
        P(along),
        P(along),
        P(along, "branch"),
        P("branch", along),
        P(None, along, "branch"),
        P("branch", along),
        P(along, None, None, None),
        P("branch", None, along, None),
        P(),
        P(),
        P("branch"),
        P("branch"),
    )
    return jax.shard_map(
        body,
        mesh=split,
        in_specs=placed,
        out_specs=(P(None, "branch", along), P("branch", None, None, None)),
        check_vma=False,
    )
```

```python
import functools

import jax
import jax.numpy as jnp
from jax import lax
from jax.experimental import pallas as pl
from jax.experimental.pallas import tpu as pltpu
from jax.sharding import Mesh
from jax.sharding import PartitionSpec as P

HEADS = 64
KVH = 8
HD = 128
GROUP = HEADS // KVH
BLK = 512
CORES = 2
SUB = 8
LANE = 128

EPS = 1e-05
ROPE_BASE = 500000.0
FLOOR = -1e30
LOWEST = -1e29
F32 = jnp.float32
BF16 = jnp.bfloat16
AXES = ("z", "core", "branch")


def ceil_div(a, b):
    return -(-a // b)


def whole(shape):
    return pl.BlockSpec(shape, lambda *_: (0,) * len(shape))


def exchange(x, axes):
    return lax.all_to_all(x, axes, split_axis=0, concat_axis=0, tiled=True)


def params(mib):
    return pltpu.CompilerParams(vmem_limit_bytes=mib * 2**20)


IN_HBM = pl.BlockSpec(memory_space=pltpu.HBM)
IN_VMEM = pl.BlockSpec(memory_space=pltpu.VMEM)
IN_SMEM = pl.BlockSpec(memory_space=pltpu.SMEM)


def bits(n):
    return [1 << i for i in range(n.bit_length() - 1)]


def mirror(q, n):
    out = 0
    top = n.bit_length() - 2
    for i in range(top + 1):
        out = out + (((q >> i) & 1) << (top - i))
    return out


def swap(x, axis, bit):
    return lax.ppermute(x, axis, [(i, i ^ bit) for i in range(lax.axis_size(axis))])


def reduce_rounds(x, axis, order):
    for bit in order:
        half = x.shape[0] // 2
        x = x[:half] + swap(x[half:], axis, bit)
    return x[0]


def gather_rounds(x, axis, order):
    x = x[None]
    for bit in order:
        x = jnp.concatenate([x, swap(x, axis, bit)], axis=0)
    return x


def add_round(x, axis, order):
    for bit in order:
        half = x.shape[0] // 2
        kept = x[:half].astype(F32)
        kept = kept + swap(x[half:], axis, bit).astype(F32)
        x = kept.astype(BF16)
    return kept[0]


def add(a, b):
    return (a.astype(F32) + b.astype(F32)).astype(BF16)


def norm_and_gather(x, gain, width):
    value = x.astype(F32)
    squares = jnp.sum(value * value, axis=2)
    squares = squares + swap(squares, "core", 1)
    for bit in bits(lax.axis_size("z")):
        squares = squares + swap(squares, "z", bit)
    scale = lax.rsqrt(squares / width + EPS)
    normed = (value * scale[..., None] * gain).astype(BF16)
    rows = gather_rounds(normed, "branch", bits(lax.axis_size("branch")))
    return rows.reshape(-1, x.shape[2])


def gather_prefix(x):
    x = gather_rounds(x, "z", bits(lax.axis_size("z"))[::-1])
    x = gather_rounds(x, "core", [1])
    return x.reshape((-1,) + x.shape[2:])


def place_table():
    z_count = lax.axis_size("z")
    owner = jnp.arange(z_count * CORES, dtype=jnp.int32)
    far = mirror((owner // CORES) ^ lax.axis_index("z"), z_count)
    return (((owner % CORES) ^ lax.axis_index("core")) * z_count + far).astype(jnp.int32)


def streamed(count, ahead, copies, work):
    for i in range(min(ahead, count)):
        for c in copies(i):
            c.start()

    def step(i, carry):
        for c in copies(i):
            c.wait()

        @pl.when(i + ahead < count)
        def _():
            for c in copies(i + ahead):
                c.start()

        work(i)
        return carry

    lax.fori_loop(0, count, step, 0)


def qkv_kernel(steps, heads_step, tiles, ids, lhs, w, out, buffer, sems):
    count = buffer.shape[0]
    columns = heads_step * HD
    branches = out.shape[2]

    def copies(i):
        at = pl.multiple_of(i * columns, columns)
        return [pltpu.make_async_copy(w.at[:, pl.ds(at, columns)], buffer.at[i], sems.at[i])]

    def work(i):
        acc = jnp.dot(lhs[...], buffer[i], preferred_element_type=F32)
        for hh in range(heads_step):
            for s in range(steps):
                index = (i * heads_step + hh) * steps + s
                owner = index // tiles
                side = (owner % CORES) ^ ids[1]
                for k in range(branches):
                    row = (k * steps + s) * SUB
                    out[side, owner // CORES, ids[2] ^ k, index % tiles] = acc[
                        row : row + SUB, hh * HD : (hh + 1) * HD
                    ]

    streamed(count, min(4, count), copies, work)


def project_qkv(ids, lhs, w, steps, z_count, branches):
    depth, columns = w.shape
    heads = columns // HD
    heads_step = max(n for n in range(1, 5) if heads % n == 0)
    count = heads // heads_step
    tiles = ceil_div(heads * steps, z_count * CORES)
    shape = (CORES, z_count, branches, tiles, SUB, HD)
    return pl.pallas_call(
        functools.partial(qkv_kernel, steps, heads_step, tiles),
        in_specs=[IN_SMEM, IN_VMEM, IN_HBM],
        out_shape=jax.ShapeDtypeStruct(shape, F32),
        scratch_shapes=[
            pltpu.VMEM((count, depth, heads_step * HD), BF16),
            pltpu.SemaphoreType.DMA((count,)),
        ],
        compiler_params=params(62),
        name="qkv",
    )(ids, lhs, w)


def gate_up_kernel(unit, start, ids, lhs, w, out, buffer, sems):
    count = buffer.shape[0]
    part = buffer.shape[3]
    z_count = out.shape[1]

    def copies(i):
        at = pl.multiple_of(i * unit + start, LANE)
        return [
            pltpu.make_async_copy(w.at[g, :, pl.ds(at, part)], buffer.at[i, g], sems.at[i, g])
            for g in range(2)
        ]

    def work(i):
        side = (i % CORES) ^ ids[1]
        far = mirror((i // CORES) ^ ids[0], z_count)
        for g in range(2):
            product = jnp.dot(lhs[...], buffer[i, g], preferred_element_type=F32)
            out[side, far, g] = product.astype(BF16)

    streamed(count, 3, copies, work)


def project_gate_up(ids, lhs, w, unit, start, part, z_count):
    rows = lhs.shape[0]
    _, depth, columns = w.shape
    count = columns // unit
    shape = (CORES, z_count, 2, rows, part)
    return pl.pallas_call(
        functools.partial(gate_up_kernel, unit, start),
        in_specs=[IN_SMEM, IN_VMEM, IN_HBM],
        out_shape=jax.ShapeDtypeStruct(shape, BF16),
        scratch_shapes=[
            pltpu.VMEM((count, 2, depth, part), BF16),
            pltpu.SemaphoreType.DMA((count, 2)),
        ],
        compiler_params=params(52),
        name="gate_up",
    )(ids, lhs, w)


def mix_kernel(steps, table, attended, w, out, lhs, buffer, sems):
    count = buffer.shape[0]
    unit = buffer.shape[2]
    tiles = attended.shape[2]

    def copies(i):
        at = pl.multiple_of(i * unit, LANE)
        return [pltpu.make_async_copy(w.at[:, pl.ds(at, unit)], buffer.at[i], sems.at[i])]

    def build():
        for j in range(lhs.shape[1] // HD):
            column = []
            for b in range(out.shape[0]):
                for s in range(steps):
                    index = j * steps + s
                    tile = attended[table[index // tiles], b, index % tiles]
                    column.append(tile.astype(F32))
            lhs[:, j * HD : (j + 1) * HD] = jnp.concatenate(column, axis=0).astype(BF16)

    for i in range(count):
        copies(i)[0].start()
    build()

    def step(i, carry):
        copies(i)[0].wait()
        acc = jnp.dot(lhs[...], buffer[i], preferred_element_type=F32)
        at = pl.ds(pl.multiple_of(i * unit, LANE), unit)
        for b in range(out.shape[0]):
            for s in range(steps):
                row = (b * steps + s) * SUB
                out[b, s, :, at] = acc[row : row + SUB].astype(BF16)
        return carry

    lax.fori_loop(0, count, step, 0)


def mix_heads(table, attended, w, steps):
    branches = attended.shape[1]
    depth, columns = w.shape
    unit = min(columns, 256)
    count = columns // unit
    rows = branches * steps * SUB
    return pl.pallas_call(
        functools.partial(mix_kernel, steps),
        in_specs=[IN_SMEM, IN_VMEM, IN_HBM],
        out_shape=jax.ShapeDtypeStruct((branches, steps, SUB, columns), BF16),
        scratch_shapes=[
            pltpu.VMEM((rows, depth), BF16),
            pltpu.VMEM((count, depth, unit), BF16),
            pltpu.SemaphoreType.DMA((count,)),
        ],
        compiler_params=params(62),
        name="mix",
    )(table, attended, w)


def down_kernel(unit, start, table, activation, w, out, buffer, sems):
    part = buffer.shape[1]
    out[...] = jnp.zeros_like(out)

    def copies(i):
        at = pl.multiple_of(i * unit + start, LANE)
        return [pltpu.make_async_copy(w.at[pl.ds(at, part), :], buffer.at[i], sems.at[i])]

    def work(i):
        out[...] += jnp.dot(activation[table[i]], buffer[i], preferred_element_type=F32)

    streamed(buffer.shape[0], min(4, buffer.shape[0]), copies, work)


def project_down(table, activation, w, unit, start):
    rows, part = activation.shape[1:]
    columns = w.shape[1]
    count = w.shape[0] // unit
    return pl.pallas_call(
        functools.partial(down_kernel, unit, start),
        in_specs=[IN_SMEM, IN_VMEM, IN_HBM],
        out_shape=jax.ShapeDtypeStruct((rows, columns), F32),
        scratch_shapes=[
            pltpu.VMEM((count, part, columns), BF16),
            pltpu.SemaphoreType.DMA((count,)),
        ],
        compiler_params=params(60),
        name="down",
    )(table, activation, w)


def prepare_kernel(steps, blocks_here, suffix_here, prefix, ids, parent, block_map, leaf, length, pos, bias):
    rows = leaf.shape[0]
    place = ids[0] * CORES + ids[1]
    sub = lax.broadcasted_iota(jnp.int32, (SUB, LANE), 0)
    base = jnp.zeros((SUB, LANE), jnp.int32)
    used = jnp.zeros((SUB, LANE), jnp.int32)
    owned = [jnp.zeros((SUB, LANE), jnp.int32) for _ in range(blocks_here)]
    for r in range(rows):
        current = leaf[r]
        depth = jnp.int32(0)
        hits = [jnp.int32(0)] * blocks_here
        for _ in range(parent.shape[0]):
            valid = current >= 0
            at = jnp.maximum(current, 0)
            slot = jnp.where(valid, block_map[at], -1)
            hits = [h + (slot == place * blocks_here + n).astype(jnp.int32) for n, h in enumerate(hits)]
            depth = depth + valid.astype(jnp.int32)
            current = jnp.where(valid, parent[at], -1)
        base = jnp.where(sub == r, BLK * depth + length[r], base)
        used = jnp.where(sub == r, length[r], used)
        owned = [jnp.where(sub == r, h, o) for h, o in zip(hits, owned)]
    tree = blocks_here * BLK
    keys = SUB * suffix_here
    sub_keys = lax.broadcasted_iota(jnp.int32, (SUB, keys), 0)
    key = lax.broadcasted_iota(jnp.int32, (SUB, keys), 1)
    suffix_ok = (key // suffix_here == sub_keys) & (
        place * suffix_here + key % suffix_here < used[:, :1]
    )
    suffix = jnp.where(suffix_ok, 0.0, FLOOR)
    lane = lax.broadcasted_iota(jnp.int32, (SUB, LANE), 1)
    for s in range(steps):
        pos[s] = (base + s).astype(F32)
        row = slice(s * SUB, (s + 1) * SUB)
        for n in range(blocks_here):
            bias[row, n * BLK : (n + 1) * BLK] = jnp.broadcast_to(
                jnp.where(owned[n][:, :1] > 0, 0.0, FLOOR), (SUB, BLK)
            )
        bias[row, tree : tree + keys] = suffix
        new_ok = (lane % SUB == sub) & (lane // SUB <= s) & (place == 0)
        bias[row, tree + keys : tree + keys + LANE] = jnp.where(new_ok, 0.0, FLOOR)


def prepare(ids, parent, block_map, leaf, length, steps, blocks_here, suffix_here, prefix):
    columns = blocks_here * BLK + SUB * suffix_here + LANE
    smem = pl.BlockSpec(memory_space=pltpu.SMEM)
    return pl.pallas_call(
        functools.partial(prepare_kernel, steps, blocks_here, suffix_here, prefix),
        in_specs=[smem] * 5,
        out_shape=[
            jax.ShapeDtypeStruct((steps, SUB, LANE), F32),
            jax.ShapeDtypeStruct((steps * SUB, columns), F32),
        ],
        name="prepare",
    )(ids, parent, block_map, leaf, length)


def attend_kernel(heads_in, tiles_in, heads_out, tiles_out, table, qkv, cosine, sine, bias, tree, suffix, out, new_kv, sums):
    k = pl.program_id(0)
    steps = cosine.shape[0]
    rows = steps * SUB
    lane = lax.broadcasted_iota(jnp.int32, (SUB, LANE), 1)

    @pl.when(k == 0)
    def _():
        sums[...] = jnp.zeros_like(sums)

    def tile(head, s):
        index = (head % heads_in) * steps + s
        return qkv[table[index // tiles_in], head // heads_in, index % tiles_in].astype(F32)

    def turned(x, s):
        return x * cosine[s] + pltpu.roll(x, HD // 2, 1) * sine[s]

    query = jnp.concatenate(
        [turned(tile(k * GROUP + g, s), s) for g in range(GROUP) for s in range(steps)], axis=0
    ).astype(BF16)
    keys = [turned(tile(HEADS + k, s), s) for s in range(steps)]
    values = [tile(HEADS + KVH + k, s) for s in range(steps)]
    for s in range(steps):
        new_kv[0, s] = keys[s].astype(BF16)
        new_kv[1, s] = values[s].astype(BF16)
    fill = [jnp.zeros((LANE - rows, HD), F32)]
    sources = [
        (tree[:, 0].reshape(-1, HD), tree[:, 1].reshape(-1, HD)),
        (suffix[:, 0].reshape(-1, HD), suffix[:, 1].reshape(-1, HD)),
        (
            jnp.concatenate(keys + fill, axis=0).astype(BF16),
            jnp.concatenate(values + fill, axis=0).astype(BF16),
        ),
    ]
    scores = []
    start = 0
    highest = jnp.full((GROUP, rows, 1), LOWEST, F32)
    for key, _ in sources:
        count = key.shape[0]
        product = lax.dot_general(
            query, key, (((1,), (1,)), ((), ())), preferred_element_type=F32
        ) * (HD**-0.5)
        product = product.reshape(GROUP, rows, count) + bias[:, start : start + count][None]
        highest = jnp.maximum(highest, jnp.max(product, axis=-1, keepdims=True))
        scores.append(product)
        start += count
    total = jnp.zeros((GROUP, rows, 1), F32)
    acc = jnp.zeros((GROUP * rows, HD), F32)
    for product, (_, value) in zip(scores, sources):
        weight = jnp.exp(product - highest)
        total = total + jnp.sum(weight, axis=-1, keepdims=True)
        acc = acc + jnp.dot(
            weight.reshape(GROUP * rows, -1).astype(BF16), value, preferred_element_type=F32
        )
    some = total > 0
    safe = jnp.where(some, total, 1.0)
    result = acc.reshape(GROUP, rows, HD) / safe
    log_sum = jnp.where(some, highest + jnp.log(safe), LOWEST)
    for g in range(GROUP):
        head = k * GROUP + g
        for s in range(steps):
            index = (head % heads_out) * steps + s
            owner, b, at = index // tiles_out, head // heads_out, index % tiles_out
            row = slice(s * SUB, (s + 1) * SUB)
            out[owner, b, at] = result[g, row].astype(BF16)
            sums[owner, b] = jnp.where(lane == at, log_sum[g, row], sums[owner, b])

    @pl.when(k == pl.num_programs(0) - 1)
    def _():
        for p in range(sums.shape[0]):
            for b in range(sums.shape[1]):
                value = sums[p, b]
                high = value.astype(BF16).astype(F32)
                rest = value - high
                middle = rest.astype(BF16).astype(F32)
                low = rest - middle
                packed = jnp.where(
                    lane < 32,
                    high,
                    jnp.where(lane < 64, pltpu.roll(middle, 32, 1), pltpu.roll(low, 64, 1)),
                )
                out[p, b, tiles_out] = packed.astype(BF16)


def attend(table, qkv, cosine, sine, bias, tree_kv, suffix_kv, heads_in, heads_out, prefix):
    _, branches, tiles_in = qkv.shape[:3]
    steps = cosine.shape[0]
    tiles_out = ceil_div(heads_out * steps, prefix)
    shape = (prefix, branches, tiles_out + 1, SUB, HD)

    def by_head(array):
        block = array.shape[:-1] + (HD,)
        return pl.BlockSpec(block, lambda k, _: (0,) * (len(block) - 1) + (k,))

    return pl.pallas_call(
        functools.partial(attend_kernel, heads_in, tiles_in, heads_out, tiles_out),
        grid_spec=pltpu.PrefetchScalarGridSpec(
            num_scalar_prefetch=1,
            grid=(KVH,),
            in_specs=[whole(a.shape) for a in (qkv, cosine, sine, bias)]
            + [by_head(tree_kv), by_head(suffix_kv)],
            out_specs=[
                whole(shape),
                pl.BlockSpec((2, steps, SUB, HD), lambda k, _: (0, 0, 0, k)),
            ],
            scratch_shapes=[pltpu.VMEM((prefix, branches, SUB, LANE), F32)],
        ),
        out_shape=[
            jax.ShapeDtypeStruct(shape, BF16),
            jax.ShapeDtypeStruct((2, steps, SUB, KVH * HD), BF16),
        ],
        compiler_params=params(62),
        name="attend",
    )(table, qkv, cosine, sine, bias, tree_kv, suffix_kv)


def join_kernel(parts, out):
    prefix, branches, count = parts.shape[:3]
    tiles = count - 1
    for b in range(branches):
        logs = []
        for p in range(prefix):
            packed = parts[p, b, tiles].astype(F32)
            logs.append(packed + pltpu.roll(packed, LANE - 32, 1) + pltpu.roll(packed, LANE - 64, 1))
        highest = functools.reduce(jnp.maximum, logs)
        weights = [jnp.exp(x - highest) for x in logs]
        total = functools.reduce(jnp.add, weights)
        weights = [w / total for w in weights]
        for t in range(tiles):
            acc = jnp.zeros((SUB, HD), F32)
            for p in range(prefix):
                acc = acc + parts[p, b, t].astype(F32) * weights[p][:, t : t + 1]
            out[b, t] = acc.astype(BF16)


def join(parts):
    _, branches, count = parts.shape[:3]
    return pl.pallas_call(
        join_kernel,
        in_specs=[IN_VMEM],
        out_specs=IN_VMEM,
        out_shape=jax.ShapeDtypeStruct((branches, count - 1, SUB, HD), BF16),
        name="join",
    )(parts)


def body(
    hidden,
    attn_gain,
    ffn_gain,
    w_qkv,
    w_out,
    w_gate_up,
    w_down,
    tree_kv,
    suffix_kv,
    parent,
    block_map,
    leaf,
    suffix_len,
):
    steps, rows, width_dev = hidden.shape
    z_count = lax.axis_size("z")
    branches = lax.axis_size("branch")
    prefix = z_count * CORES
    devices = prefix * branches
    width = width_dev * prefix
    near = bits(z_count)
    across = bits(branches)
    table = place_table()
    ids = jnp.stack([lax.axis_index(a) for a in AXES]).astype(jnp.int32)

    pos, bias = prepare(
        ids, parent, block_map, leaf, suffix_len, steps, tree_kv.shape[0], suffix_kv.shape[2], prefix
    )
    half = HD // 2
    frequency = ROPE_BASE ** (-(jnp.arange(half, dtype=F32) * 2.0 / HD))
    angles = pos[..., :1] * frequency
    cos, sin = jnp.cos(angles), jnp.sin(angles)
    cosine = jnp.concatenate([cos, cos], axis=-1)
    sine = jnp.concatenate([-sin, sin], axis=-1)

    lhs = norm_and_gather(hidden, attn_gain, width)
    part_sums = project_qkv(ids, lhs, w_qkv, steps, z_count, branches)
    chip_sums = part_sums[0] + swap(part_sums[1], "core", 1)
    tiles = chip_sums.shape[2]
    received = exchange(chip_sums.reshape(z_count * branches, tiles, SUB, HD), ("z", "branch"))
    summed = jnp.sum(received.reshape(z_count, branches, tiles, SUB, HD), axis=0).astype(BF16)
    qkv = gather_prefix(summed)

    heads_in = w_qkv.shape[1] // HD
    heads_out = w_out.shape[0] // HD
    softmax_parts, new_kv = attend(
        table, qkv, cosine, sine, bias, tree_kv, suffix_kv, heads_in, heads_out, prefix
    )
    new_kv = new_kv.transpose(2, 0, 1, 3)
    tiles_out = softmax_parts.shape[2]
    received = exchange(softmax_parts.reshape(devices, tiles_out, SUB, HD), AXES)
    attended = join(received.reshape(prefix, branches, tiles_out, SUB, HD))
    attended = gather_prefix(attended)

    mixed = exchange(mix_heads(table, attended, w_out, steps), "branch")
    mixed = jnp.sum(mixed.astype(F32), axis=0)
    residual = (hidden.astype(F32) + mixed).astype(BF16)

    lhs = norm_and_gather(residual, ffn_gain, width)
    unit = ceil_div(w_gate_up.shape[2] // LANE, prefix) * LANE
    first = ceil_div(unit // LANE, 2) * LANE
    down = None
    for start, part in ((0, first), (first, unit - first)):
        if part == 0:
            continue
        part_sums = project_gate_up(ids, lhs, w_gate_up, unit, start, part, z_count)
        chip_sums = add(part_sums[0], swap(part_sums[1], "core", 1))
        lhs, chip_sums = lax.optimization_barrier((lhs, chip_sums))
        gate, up = add_round(chip_sums, "z", near)
        activation = gather_prefix((jax.nn.silu(gate) * up).astype(BF16))
        product = project_down(table, activation, w_down, unit, start)
        down = product if down is None else down + product
    down = down.astype(BF16).reshape(branches, steps, rows, width_dev)
    down = add_round(down, "branch", across[::-1])
    result = (residual.astype(F32) + down).astype(BF16)
    return (result, new_kv)


def solution(mesh):
    prefix, branches = mesh.shape["prefix"], mesh.shape["branch"]
    split = Mesh(mesh.devices.reshape(prefix // CORES, CORES, branches), AXES)
    along = ("z", "core")
    placed = (
        P(None, "branch", along),
        P(along),
        P(along),
        P(along, "branch"),
        P("branch", along),
        P(None, along, "branch"),
        P("branch", along),
        P(along, None, None, None),
        P("branch", None, along, None),
        P(),
        P(),
        P("branch"),
        P("branch"),
    )
    return jax.shard_map(
        body,
        mesh=split,
        in_specs=placed,
        out_specs=(P(None, "branch", along), P("branch", None, None, None)),
        check_vma=False,
    )
```

```python
import functools

import jax
import jax.numpy as jnp
import numpy as np
from jax import lax
from jax.experimental import pallas as pl
from jax.experimental.pallas import tpu as pltpu
from jax.sharding import Mesh
from jax.sharding import PartitionSpec as P

HEADS = 64
KVH = 8
HD = 128
GROUP = HEADS // KVH
BLK = 512
CORES = 2
SUB = 8
LANE = 128

EPS = 1e-05
ROPE_BASE = 500000.0
FLOOR = -1e30
LOWEST = -1e29
F32 = jnp.float32
BF16 = jnp.bfloat16
AXES = ("z", "core", "branch")


def ceil_div(a, b):
    return -(-a // b)


def whole(shape):
    return pl.BlockSpec(shape, lambda *_: (0,) * len(shape))


def cost(rows, w):
    return pl.CostEstimate(
        flops=2 * rows * w[0] * w[1], bytes_accessed=2 * w[0] * w[1], transcendentals=0
    )


def exchange(x, axes):
    return lax.all_to_all(x, axes, split_axis=0, concat_axis=0, tiled=True)


def params(mib):
    return pltpu.CompilerParams(vmem_limit_bytes=mib * 2**20)


IN_HBM = pl.BlockSpec(memory_space=pltpu.HBM)
IN_VMEM = pl.BlockSpec(memory_space=pltpu.VMEM)
IN_SMEM = pl.BlockSpec(memory_space=pltpu.SMEM)


def bits(n):
    return [1 << i for i in range(n.bit_length() - 1)]


def mirror(q, n):
    out = 0
    top = n.bit_length() - 2
    for i in range(top + 1):
        out = out + (((q >> i) & 1) << (top - i))
    return out


def swap(x, axis, bit):
    return lax.ppermute(x, axis, [(i, i ^ bit) for i in range(lax.axis_size(axis))])


def reduce_rounds(x, axis, order):
    for bit in order:
        half = x.shape[0] // 2
        x = x[:half] + swap(x[half:], axis, bit)
    return x[0]


def gather_rounds(x, axis, order):
    x = x[None]
    for bit in order:
        x = jnp.concatenate([x, swap(x, axis, bit)], axis=0)
    return x


def add_round(x, axis, order):
    for bit in order:
        half = x.shape[0] // 2
        kept = x[:half].astype(F32)
        kept = kept + swap(x[half:], axis, bit).astype(F32)
        x = kept.astype(BF16)
    return kept[0]


def add(a, b):
    return (a.astype(F32) + b.astype(F32)).astype(BF16)


def as_tile(x):
    return jnp.pad(x, ((0, -x.shape[0] % SUB), (0, LANE - x.shape[1])))


def normed(x, squares, gain, width):
    scale = lax.rsqrt(squares / width + EPS)
    return (x * scale[..., None] * gain).astype(BF16)


def norm_rows(x, gain, width):
    value = x.astype(F32)
    squares = jnp.sum(value * value, axis=3)
    total = as_tile(squares.reshape(-1, squares.shape[-1]))
    total = total + swap(total, "core", 1)
    for bit in bits(lax.axis_size("z")):
        total = total + swap(total, "z", bit)
    total = total[: squares.shape[0] * squares.shape[1], : squares.shape[2]].reshape(squares.shape)
    return normed(value, total, gain, width).reshape(-1, x.shape[3])


def sum_round(x, bit):
    other = swap(x, "branch", bit).astype(F32)
    shape = other.shape
    other = jnp.flip(other.reshape((shape[0] // (2 * bit), 2, bit) + shape[1:]), axis=1)
    return x.astype(F32) + other.reshape(shape)


def sum_branches(first, second):
    order = bits(lax.axis_size("branch"))
    for one, two in zip(order, order[::-1]):
        first, second = sum_round(first.astype(BF16), one), sum_round(second.astype(BF16), two)
    return jnp.concatenate([first, second], axis=-1)


def own_sum(x):
    n = x.shape[0]
    if n > 4:
        return add_round(x, "branch", bits(n)[::-1])
    arrived = [swap(x[k], "branch", k) for k in range(1, n)]
    return functools.reduce(jnp.add, [a.astype(F32) for a in [x[0]] + arrived])


def gather_prefix(x):
    x = gather_rounds(x, "z", bits(lax.axis_size("z"))[::-1])
    x = gather_rounds(x, "core", [1])
    return x.reshape((-1,) + x.shape[2:])


def place_table():
    z_count = lax.axis_size("z")
    owner = jnp.arange(z_count * CORES, dtype=jnp.int32)
    far = mirror((owner // CORES) ^ lax.axis_index("z"), z_count)
    return (((owner % CORES) ^ lax.axis_index("core")) * z_count + far).astype(jnp.int32)


def key_head(head):
    return head // GROUP if head < HEADS else (head - HEADS) % KVH


def ranks(heads_each, branches):
    rank, most = {}, 0
    for b in range(branches):
        count = [0] * CORES
        for head in range(b * heads_each, (b + 1) * heads_each):
            core = key_head(head) % CORES
            rank[head] = count[core]
            count[core] += 1
        most = max(most, *count)
    return rank, most


def head_tables(steps, z_count, branches):
    heads_in = (HEADS + 2 * KVH) // branches
    heads_out = HEADS // branches
    rank_in, most = ranks(heads_in, branches)
    tiles_in = ceil_div(most * steps, z_count)
    rank_out, most = ranks(heads_out, branches)
    tiles_out = ceil_div(most * steps, z_count)
    kv_core = KVH // CORES
    project = np.zeros((branches, heads_in), np.int32)
    for head, rank in rank_in.items():
        project[head // heads_in, head % heads_in] = rank * steps * CORES + key_head(head) % CORES
    fetch = np.zeros((z_count, CORES, kv_core, GROUP + 2, steps), np.int32)
    send = np.zeros((CORES, kv_core, GROUP, steps), np.int32)
    mix = np.zeros((z_count, CORES, branches, heads_out, steps), np.int32)
    for s in range(steps):
        for core in range(CORES):
            for j in range(kv_core):
                key = j * CORES + core
                heads = [key * GROUP + g for g in range(GROUP)] + [HEADS + key, HEADS + KVH + key]
                for n, head in enumerate(heads):
                    chip, tile = divmod(rank_in[head] * steps + s, tiles_in)
                    for z in range(z_count):
                        row = mirror(chip ^ z, z_count) * branches + head // heads_in
                        fetch[z, core, j, n, s] = row * tiles_in + tile
                    if head < HEADS:
                        chip, tile = divmod(rank_out[head] * steps + s, tiles_out)
                        row = chip * branches + head // heads_out
                        send[core, j, n, s] = row * LANE + tile
        for head, rank in rank_out.items():
            chip, tile = divmod(rank * steps + s, tiles_out)
            for z in range(z_count):
                for core in range(CORES):
                    side = (key_head(head) % CORES) ^ core
                    row = side * z_count + mirror(chip ^ z, z_count)
                    mix[z, core, head // heads_out, head % heads_out, s] = row * LANE + tile
    full = (z_count, CORES, branches)
    parts = [
        np.broadcast_to(project[None, None], full + project.shape[1:]),
        np.broadcast_to(fetch.reshape(z_count, CORES, 1, -1), full + (fetch[0, 0].size,)),
        np.broadcast_to(send.reshape(1, CORES, 1, -1), full + (send[0].size,)),
        mix.reshape(full + (-1,)),
    ]
    starts = np.cumsum([0] + [p.shape[-1] for p in parts]).tolist()
    return tiles_in, tiles_out, np.concatenate(parts, axis=-1), starts


def streamed(count, ahead, copies, work):
    for i in range(min(ahead, count)):
        for c in copies(i):
            c.start()

    def step(i, carry):
        for c in copies(i):
            c.wait()

        @pl.when(i + ahead < count)
        def _():
            for c in copies(i + ahead):
                c.start()

        work(i)
        return carry

    lax.fori_loop(0, count, step, 0)


def qkv_kernel(steps, heads_step, tiles, ids, table, lhs, w, out):
    columns = heads_step * HD
    branches = out.shape[2]
    for i in range(w.shape[1] // columns):
        acc = jnp.dot(
            lhs[...], w[:, i * columns : (i + 1) * columns], preferred_element_type=F32
        )
        for hh in range(heads_step):
            code = table[i * heads_step + hh]
            side = (code % CORES) ^ ids[1]
            for s in range(steps):
                index = code // CORES + s
                for k in range(branches):
                    row = (k * steps + s) * SUB
                    out[side, index // tiles, ids[2] ^ k, index % tiles] = acc[
                        row : row + SUB, hh * HD : (hh + 1) * HD
                    ]


def project_qkv(ids, table, lhs, w, steps, z_count, branches, tiles):
    heads = w.shape[1] // HD
    heads_step = max(n for n in range(1, 5) if heads % n == 0)
    shape = (CORES, z_count, branches, tiles, SUB, HD)
    return pl.pallas_call(
        functools.partial(qkv_kernel, steps, heads_step, tiles),
        in_specs=[IN_SMEM, IN_SMEM, IN_VMEM, IN_VMEM],
        out_shape=jax.ShapeDtypeStruct(shape, F32),
        compiler_params=params(24),
        cost_estimate=cost(lhs.shape[0], w.shape),
        name="qkv",
    )(ids, table, lhs, w)


def gate_up_kernel(unit, start, ids, lhs, w, out, buffer, sems):
    count = buffer.shape[0]
    part = buffer.shape[3]
    z_count = out.shape[1]

    def copies(i):
        at = pl.multiple_of(i * unit + start, LANE)
        return [
            pltpu.make_async_copy(w.at[g, :, pl.ds(at, part)], buffer.at[i, g], sems.at[i, g])
            for g in range(2)
        ]

    def work(i):
        side = (i % CORES) ^ ids[1]
        far = mirror((i // CORES) ^ ids[0], z_count)
        for g in range(2):
            product = jnp.dot(lhs[...], buffer[i, g], preferred_element_type=F32)
            out[side, far, g] = product.astype(BF16)

    streamed(count, 3, copies, work)


def project_gate_up(ids, lhs, w, unit, start, part, z_count):
    rows = lhs.shape[0]
    _, depth, columns = w.shape
    count = columns // unit
    shape = (CORES, z_count, 2, rows, part)
    return pl.pallas_call(
        functools.partial(gate_up_kernel, unit, start),
        in_specs=[IN_SMEM, IN_VMEM, IN_HBM],
        out_shape=jax.ShapeDtypeStruct(shape, BF16),
        scratch_shapes=[
            pltpu.VMEM((count, 2, depth, part), BF16),
            pltpu.SemaphoreType.DMA((count, 2)),
        ],
        compiler_params=params(32),
        cost_estimate=cost(rows, (depth, 2 * count * part)),
        name="gate_up",
    )(ids, lhs, w)


def mix_kernel(steps, base, ids, table, attended, w, first, second, lhs):
    unit = min(first.shape[3], 256)
    count = w.shape[1] // unit
    for j in range(lhs.shape[1] // HD):
        codes = [table[base + j * steps + s] for s in range(steps)]
        column = [
            attended[code // LANE, ids[2] ^ k, code % LANE].astype(F32)
            for k in range(first.shape[0])
            for code in codes
        ]
        lhs[:, j * HD : (j + 1) * HD] = jnp.concatenate(column, axis=0).astype(BF16)
    for i in range(count):
        acc = jnp.dot(lhs[...], w[:, i * unit : (i + 1) * unit], preferred_element_type=F32)
        out = first if i < count // 2 else second
        at = slice(i % (count // 2) * unit, (i % (count // 2) + 1) * unit)
        out[:, :, :, at] = acc.reshape(out.shape[:3] + (unit,)).astype(BF16)


def mix_heads(ids, table, base, attended, w, steps):
    branches = attended.shape[1]
    depth, columns = w.shape
    rows = branches * steps * SUB
    half = jax.ShapeDtypeStruct((branches, steps, SUB, columns // 2), BF16)
    return pl.pallas_call(
        functools.partial(mix_kernel, steps, base),
        in_specs=[IN_SMEM, IN_SMEM, IN_VMEM, IN_VMEM],
        out_shape=[half, half],
        scratch_shapes=[pltpu.VMEM((rows, depth), BF16)],
        compiler_params=params(24),
        cost_estimate=cost(rows, w.shape),
        name="mix",
    )(ids, table, attended, w)


def down_kernel(unit, start, table, *refs):
    *prior, activation, w, out, acc, buffer, sems = refs
    part = buffer.shape[1]
    acc[...] = prior[0][...] if prior else jnp.zeros_like(acc)

    def copies(i):
        at = pl.multiple_of(i * unit + start, LANE)
        return [pltpu.make_async_copy(w.at[pl.ds(at, part), :], buffer.at[i], sems.at[i])]

    def work(i):
        acc[...] += jnp.dot(activation[table[i]], buffer[i], preferred_element_type=F32)

    streamed(buffer.shape[0], min(6, buffer.shape[0]), copies, work)
    out[...] = acc[...].reshape(out.shape).astype(out.dtype)


def project_down(table, prior, activation, w, unit, start, shape):
    rows, part = activation.shape[1:]
    columns = w.shape[1]
    count = w.shape[0] // unit
    last = shape is not None
    result = (shape, BF16) if last else ((rows, columns), F32)
    return pl.pallas_call(
        functools.partial(down_kernel, unit, start),
        in_specs=[IN_SMEM] + [IN_VMEM] * (len(prior) + 1) + [IN_HBM],
        out_specs=IN_VMEM,
        out_shape=jax.ShapeDtypeStruct(*result),
        scratch_shapes=[
            pltpu.VMEM((rows, columns), F32),
            pltpu.VMEM((count, part, columns), BF16),
            pltpu.SemaphoreType.DMA((count,)),
        ],
        compiler_params=params(52),
        cost_estimate=cost(rows, (count * part, columns)),
        name="down",
    )(table, *prior, activation, w)


def prepare_kernel(steps, blocks_here, suffix_here, ids, parent, block_map, leaf, length, pos, bias):
    rows = leaf.shape[0]
    places = [ids[0] * CORES + (ids[1] ^ side) for side in range(CORES)]
    slots = [place * blocks_here + n for place in places for n in range(blocks_here)]
    sub = lax.broadcasted_iota(jnp.int32, (SUB, LANE), 0)
    base = jnp.zeros((SUB, LANE), jnp.int32)
    used = jnp.zeros((SUB, LANE), jnp.int32)
    owned = [jnp.zeros((SUB, LANE), jnp.int32) for _ in slots]
    for r in range(rows):
        current = leaf[r]
        depth = jnp.int32(0)
        hits = [jnp.int32(0)] * len(slots)
        for _ in range(parent.shape[0]):
            valid = current >= 0
            at = jnp.maximum(current, 0)
            found = jnp.where(valid, block_map[at], -1)
            hits = [h + (found == slot).astype(jnp.int32) for slot, h in zip(slots, hits)]
            depth = depth + valid.astype(jnp.int32)
            current = jnp.where(valid, parent[at], -1)
        base = jnp.where(sub == r, BLK * depth + length[r], base)
        used = jnp.where(sub == r, length[r], used)
        owned = [jnp.where(sub == r, h, o) for h, o in zip(hits, owned)]
    keys = SUB * suffix_here
    key_row = lax.broadcasted_iota(jnp.int32, (SUB, keys), 0)
    key = lax.broadcasted_iota(jnp.int32, (SUB, keys), 1)
    columns = [
        jnp.broadcast_to(jnp.where(o[:, :1] > 0, 0.0, FLOOR), (SUB, BLK)) for o in owned
    ]
    for place in places:
        ok = (key // suffix_here == key_row) & (
            place * suffix_here + key % suffix_here < used[:, :1]
        )
        columns.append(jnp.where(ok, 0.0, FLOOR))
    shared = jnp.concatenate(columns, axis=1)
    start = shared.shape[1]
    lane = lax.broadcasted_iota(jnp.int32, (SUB, LANE), 1)
    for s in range(steps):
        pos[s] = (base + s).astype(F32)
        row = slice(s * SUB, (s + 1) * SUB)
        bias[row, :start] = shared
        new_ok = (lane % SUB == sub) & (lane // SUB <= s) & (ids[0] == 0)
        bias[row, start : start + LANE] = jnp.where(new_ok, 0.0, FLOOR)


def prepare(ids, parent, block_map, leaf, length, steps, blocks_here, suffix_here):
    columns = CORES * (blocks_here * BLK + SUB * suffix_here) + LANE
    return pl.pallas_call(
        functools.partial(prepare_kernel, steps, blocks_here, suffix_here),
        in_specs=[IN_SMEM] * 5,
        out_specs=[IN_VMEM, IN_VMEM],
        out_shape=[
            jax.ShapeDtypeStruct((steps, SUB, LANE), F32),
            jax.ShapeDtypeStruct((steps * SUB, columns), F32),
        ],
        cost_estimate=pl.CostEstimate(flops=2**22, bytes_accessed=2**20, transcendentals=0),
        name="prepare",
    )(ids, parent, block_map, leaf, length)


def attend_kernel(
    fetch, send, table, qkv, cosine, sine, bias, tree, tree_two, suffix, suffix_two, out, new_kv, sums
):
    steps = cosine.shape[0]
    rows = steps * SUB
    tiles_out = out.shape[1] - 1
    kv_core = KVH // CORES
    lane = lax.broadcasted_iota(jnp.int32, (SUB, LANE), 1)
    sums[...] = jnp.zeros_like(sums)

    def turned(x, s):
        return x * cosine[s] + pltpu.roll(x, HD // 2, 1) * sine[s]

    for j in range(kv_core):

        def tile(n, s):
            return qkv[table[fetch + (j * (GROUP + 2) + n) * steps + s]].astype(F32)

        query = jnp.concatenate(
            [turned(tile(g, s), s) for g in range(GROUP) for s in range(steps)], axis=0
        ).astype(BF16)
        keys = [turned(tile(GROUP, s), s) for s in range(steps)]
        values = [tile(GROUP + 1, s) for s in range(steps)]
        at = slice(j * HD, (j + 1) * HD)
        for s in range(steps):
            new_kv[0, s, :, at] = keys[s].astype(BF16)
            new_kv[1, s, :, at] = values[s].astype(BF16)
        fill = [jnp.zeros((LANE - rows, HD), F32)]
        sources = [
            (kv[:, 0, :, at].reshape(-1, HD), kv[:, 1, :, at].reshape(-1, HD))
            for kv in (tree, tree_two, suffix, suffix_two)
        ]
        sources.append(
            (
                jnp.concatenate(keys + fill, axis=0).astype(BF16),
                jnp.concatenate(values + fill, axis=0).astype(BF16),
            )
        )
        scores = []
        start = 0
        highest = jnp.full((GROUP, rows, 1), LOWEST, F32)
        for key, _ in sources:
            count = key.shape[0]
            product = lax.dot_general(
                query, key, (((1,), (1,)), ((), ())), preferred_element_type=F32
            ) * (HD**-0.5)
            product = product.reshape(GROUP, rows, count) + bias[:, start : start + count][None]
            highest = jnp.maximum(highest, jnp.max(product, axis=-1, keepdims=True))
            scores.append(product)
            start += count
        total = jnp.zeros((GROUP, rows, 1), F32)
        acc = jnp.zeros((GROUP * rows, HD), F32)
        for product, (_, value) in zip(scores, sources):
            weight = jnp.exp(product - highest)
            total = total + jnp.sum(weight, axis=-1, keepdims=True)
            acc = acc + jnp.dot(
                weight.reshape(GROUP * rows, -1).astype(BF16), value, preferred_element_type=F32
            )
        some = total > 0
        safe = jnp.where(some, total, 1.0)
        result = acc.reshape(GROUP, rows, HD) / safe
        log_sum = jnp.where(some, highest + jnp.log(safe), LOWEST)
        for g in range(GROUP):
            for s in range(steps):
                code = table[send + (j * GROUP + g) * steps + s]
                place, t = code // LANE, code % LANE
                row = slice(s * SUB, (s + 1) * SUB)
                out[place, t] = result[g, row].astype(BF16)
                sums[place] = jnp.where(lane == t, log_sum[g, row], sums[place])

    for p in range(sums.shape[0]):
        out[p, tiles_out] = pack_sums(sums[p])


def pack_sums(value):
    lane = lax.broadcasted_iota(jnp.int32, (SUB, LANE), 1)
    high = value.astype(BF16).astype(F32)
    rest = value - high
    middle = rest.astype(BF16).astype(F32)
    low = rest - middle
    lows = jnp.where(lane < 64, pltpu.roll(middle, 32, 1), pltpu.roll(low, 64, 1))
    return jnp.where(lane < 32, high, lows).astype(BF16)


def attend(table, fetch, send, qkv, cosine, sine, bias, sources, devices, tiles):
    steps = cosine.shape[0]
    kv_core = KVH // CORES
    shape = (devices, tiles + 1, SUB, HD)
    return pl.pallas_call(
        functools.partial(attend_kernel, fetch, send),
        in_specs=[IN_SMEM] + [IN_VMEM] * 8,
        out_specs=[IN_VMEM, IN_VMEM],
        out_shape=[
            jax.ShapeDtypeStruct(shape, BF16),
            jax.ShapeDtypeStruct((2, steps, SUB, kv_core * HD), BF16),
        ],
        scratch_shapes=[pltpu.VMEM((devices, SUB, LANE), F32)],
        compiler_params=params(32),
        cost_estimate=pl.CostEstimate(
            flops=2**30, bytes_accessed=2 * sum(a.size for a in sources), transcendentals=2**21
        ),
        name="attend",
    )(table, qkv, cosine, sine, bias, *sources)


def trade_heads(kv):
    heads = [kv[..., n * HD : (n + 1) * HD] for n in range(KVH)]
    even = jnp.concatenate(heads[0::CORES], axis=-1)
    odd = jnp.concatenate(heads[1::CORES], axis=-1)
    first = lax.axis_index("core") == 0
    return [jnp.where(first, even, odd), swap(jnp.where(first, odd, even), "core", 1)]


def both_cores(own):
    other = swap(own, "core", 1)
    first = lax.axis_index("core") == 0
    even, odd = jnp.where(first, own, other), jnp.where(first, other, own)
    count = own.shape[-1] // HD
    spans = [slice(n * HD, (n + 1) * HD) for n in range(count)]
    return jnp.concatenate([x[..., at] for at in spans for x in (even, odd)], axis=-1)


def join_kernel(parts, out):
    prefix, branches, count = parts.shape[:3]
    tiles = count - 1
    for b in range(branches):
        logs = []
        for p in range(prefix):
            packed = parts[p, b, tiles].astype(F32)
            logs.append(packed + pltpu.roll(packed, LANE - 32, 1) + pltpu.roll(packed, LANE - 64, 1))
        highest = functools.reduce(jnp.maximum, logs)
        weights = [jnp.exp(x - highest) for x in logs]
        total = functools.reduce(jnp.add, weights)
        weights = [w / total for w in weights]
        for t in range(tiles):
            acc = jnp.zeros((SUB, HD), F32)
            for p in range(prefix):
                acc = acc + parts[p, b, t].astype(F32) * weights[p][:, t : t + 1]
            out[b, t] = acc.astype(BF16)


def join(parts):
    _, branches, count = parts.shape[:3]
    return pl.pallas_call(
        join_kernel,
        in_specs=[IN_VMEM],
        out_specs=IN_VMEM,
        out_shape=jax.ShapeDtypeStruct((branches, count - 1, SUB, HD), BF16),
        name="join",
    )(parts)


def body(
    hidden,
    attn_gain,
    ffn_gain,
    w_qkv,
    w_out,
    w_gate_up,
    w_down,
    tree_kv,
    suffix_kv,
    parent,
    block_map,
    leaf,
    suffix_len,
):
    steps, rows, width_dev = hidden.shape
    z_count = lax.axis_size("z")
    branches = lax.axis_size("branch")
    prefix = z_count * CORES
    width = width_dev * prefix
    near = bits(z_count)
    across = bits(branches)
    places = place_table()
    ids = jnp.stack([lax.axis_index(a) for a in AXES]).astype(jnp.int32)

    tiles_in, tiles_out, table, (_, fetch, send, mix, _) = head_tables(steps, z_count, branches)
    table = jnp.asarray(table)[tuple(lax.axis_index(a) for a in AXES)]
    pos, bias = prepare(
        ids, parent, block_map, leaf, suffix_len, steps, tree_kv.shape[0], suffix_kv.shape[2]
    )
    half = HD // 2
    frequency = ROPE_BASE ** (-(jnp.arange(half, dtype=F32) * 2.0 / HD))
    angles = pos[..., :1] * frequency
    cos, sin = jnp.cos(angles), jnp.sin(angles)
    cosine = jnp.concatenate([cos, cos], axis=-1)
    sine = jnp.concatenate([-sin, sin], axis=-1)

    every_row = gather_rounds(hidden, "branch", across)
    lhs = norm_rows(every_row, attn_gain, width)
    sources = trade_heads(tree_kv) + trade_heads(suffix_kv)
    lhs, table, sources, cosine, sine, bias = lax.optimization_barrier(
        (lhs, table, sources, cosine, sine, bias)
    )
    part_sums = project_qkv(ids, table, lhs, w_qkv, steps, z_count, branches, tiles_in)
    chip_sums = part_sums[0] + swap(part_sums[1], "core", 1)
    plane = z_count * branches
    received = exchange(chip_sums.reshape(plane, tiles_in, SUB, HD), ("z", "branch"))
    summed = jnp.sum(received.reshape(z_count, branches, tiles_in, SUB, HD), axis=0).astype(BF16)
    qkv = gather_rounds(summed, "z", near[::-1]).reshape(-1, SUB, HD)

    softmax_parts, new_kv = attend(
        table, fetch, send, qkv, cosine, sine, bias, sources, plane, tiles_out
    )
    received = exchange(softmax_parts, ("z", "branch"))
    attended = join(received.reshape(z_count, branches, tiles_out + 1, SUB, HD))
    attended = gather_prefix(attended)
    new_kv = both_cores(new_kv).transpose(2, 0, 1, 3)

    mixed = sum_branches(*mix_heads(ids, table, mix, attended, w_out, steps))
    residual = (every_row.astype(F32) + mixed).astype(BF16)
    lhs = norm_rows(residual, ffn_gain, width)

    unit = ceil_div(w_gate_up.shape[2] // LANE, prefix) * LANE
    first = ceil_div(unit // LANE, 2) * LANE
    spans = [(at, size) for at, size in ((0, first), (first, unit - first)) if size]
    down = []
    for start, part in spans:
        part_sums = project_gate_up(ids, lhs, w_gate_up, unit, start, part, z_count)
        chip_sums = add(part_sums[0], swap(part_sums[1], "core", 1))
        lhs, chip_sums = lax.optimization_barrier((lhs, chip_sums))
        gate, up = add_round(chip_sums, "z", near)
        activation = gather_prefix((jax.nn.silu(gate) * up).astype(BF16))
        shape = (branches, steps, rows, width_dev) if start == spans[-1][0] else None
        down = [project_down(places, down, activation, w_down, unit, start, shape)]
    result = (residual[0].astype(F32) + own_sum(down[0])).astype(BF16)
    return (result, new_kv)


def solution(mesh):
    prefix, branches = mesh.shape["prefix"], mesh.shape["branch"]
    split = Mesh(mesh.devices.reshape(prefix // CORES, CORES, branches), AXES)
    along = ("z", "core")
    placed = (
        P(None, "branch", along),
        P(along),
        P(along),
        P(along, "branch"),
        P("branch", along),
        P(None, along, "branch"),
        P("branch", along),
        P(along, None, None, None),
        P("branch", None, along, None),
        P(),
        P(),
        P("branch"),
        P("branch"),
    )
    return jax.shard_map(
        body,
        mesh=split,
        in_specs=placed,
        out_specs=(P(None, "branch", along), P("branch", None, None, None)),
        check_vma=False,
    )
```

```python
import functools

import jax
import jax.numpy as jnp
import numpy as np
from jax import lax
from jax.experimental import pallas as pl
from jax.experimental.pallas import tpu as pltpu
from jax.sharding import Mesh
from jax.sharding import PartitionSpec as P

HEADS = 64
KVH = 8
HD = 128
GROUP = HEADS // KVH
BLK = 512
CORES = 2
SUB = 8
LANE = 128

EPS = 1e-05
ROPE_BASE = 500000.0
FLOOR = -1e30
LOWEST = -1e29
F32 = jnp.float32
BF16 = jnp.bfloat16
AXES = ("z", "core", "branch")


def ceil_div(a, b):
    return -(-a // b)


def whole(shape):
    return pl.BlockSpec(shape, lambda *_: (0,) * len(shape))


def cost(rows, w):
    return pl.CostEstimate(
        flops=2 * rows * w[0] * w[1], bytes_accessed=2 * w[0] * w[1], transcendentals=0
    )


def exchange(x, axes):
    return lax.all_to_all(x, axes, split_axis=0, concat_axis=0, tiled=True)


def params(mib):
    return pltpu.CompilerParams(vmem_limit_bytes=mib * 2**20)


IN_HBM = pl.BlockSpec(memory_space=pltpu.HBM)
IN_VMEM = pl.BlockSpec(memory_space=pltpu.VMEM)
IN_SMEM = pl.BlockSpec(memory_space=pltpu.SMEM)


def bits(n):
    return [1 << i for i in range(n.bit_length() - 1)]


def mirror(q, n):
    out = 0
    top = n.bit_length() - 2
    for i in range(top + 1):
        out = out + (((q >> i) & 1) << (top - i))
    return out


def swap(x, axis, bit):
    return lax.ppermute(x, axis, [(i, i ^ bit) for i in range(lax.axis_size(axis))])


def reduce_rounds(x, axis, order):
    for bit in order:
        half = x.shape[0] // 2
        x = x[:half] + swap(x[half:], axis, bit)
    return x[0]


def gather_rounds(x, axis, order):
    x = x[None]
    for bit in order:
        x = jnp.concatenate([x, swap(x, axis, bit)], axis=0)
    return x


def gather(x, axis):
    n = lax.axis_size(axis)
    if n > 4:
        return gather_rounds(x, axis, bits(n))
    return jnp.stack([x] + [swap(x, axis, k) for k in range(1, n)])


def total_along(x, axis):
    n = lax.axis_size(axis)
    if n > 4:
        for bit in bits(n):
            x = x + swap(x, axis, bit)
        return x
    return functools.reduce(jnp.add, [x] + [swap(x, axis, k) for k in range(1, n)])


def add_round(x, axis, order):
    for bit in order:
        half = x.shape[0] // 2
        kept = x[:half].astype(F32)
        kept = kept + swap(x[half:], axis, bit).astype(F32)
        x = kept.astype(BF16)
    return kept[0]


def add(a, b):
    return (a.astype(F32) + b.astype(F32)).astype(BF16)


def as_tile(x):
    return jnp.pad(x, ((0, -x.shape[0] % SUB), (0, LANE - x.shape[1])))


def normed(x, squares, gain, width):
    scale = lax.rsqrt(squares / width + EPS)
    return (x * scale[..., None] * gain).astype(BF16)


def norm_rows(x, gain, width):
    value = x.astype(F32)
    squares = jnp.sum(value * value, axis=3)
    total = as_tile(squares.reshape(-1, squares.shape[-1]))
    total = total + swap(total, "core", 1)
    total = total_along(total, "z")
    total = total[: squares.shape[0] * squares.shape[1], : squares.shape[2]].reshape(squares.shape)
    return normed(value, total, gain, width).reshape(-1, x.shape[3])


def sum_round(x, bit):
    other = swap(x, "branch", bit).astype(F32)
    shape = other.shape
    other = jnp.flip(other.reshape((shape[0] // (2 * bit), 2, bit) + shape[1:]), axis=1)
    return x.astype(F32) + other.reshape(shape)


def sum_branches(first, second):
    order = bits(lax.axis_size("branch"))
    for one, two in zip(order, order[::-1]):
        first, second = sum_round(first.astype(BF16), one), sum_round(second.astype(BF16), two)
    return jnp.concatenate([first, second], axis=-1)


def own_sum(x):
    n = x.shape[0]
    if n > 4:
        return add_round(x, "branch", bits(n)[::-1])
    arrived = [swap(x[k], "branch", k) for k in range(1, n)]
    return functools.reduce(jnp.add, [a.astype(F32) for a in [x[0]] + arrived])


def gather_prefix(x):
    x = gather_rounds(x, "z", bits(lax.axis_size("z"))[::-1])
    x = gather_rounds(x, "core", [1])
    return x.reshape((-1,) + x.shape[2:])


def place_table():
    z_count = lax.axis_size("z")
    owner = jnp.arange(z_count * CORES, dtype=jnp.int32)
    far = mirror((owner // CORES) ^ lax.axis_index("z"), z_count)
    return (((owner % CORES) ^ lax.axis_index("core")) * z_count + far).astype(jnp.int32)


def key_head(head):
    return head // GROUP if head < HEADS else (head - HEADS) % KVH


def ranks(heads_each, branches):
    rank, most = {}, 0
    for b in range(branches):
        count = [0] * CORES
        for head in range(b * heads_each, (b + 1) * heads_each):
            core = key_head(head) % CORES
            rank[head] = count[core]
            count[core] += 1
        most = max(most, *count)
    return rank, most


def head_tables(steps, z_count, branches):
    heads_in = (HEADS + 2 * KVH) // branches
    heads_out = HEADS // branches
    rank_in, most = ranks(heads_in, branches)
    tiles_in = ceil_div(most * steps, z_count)
    rank_out, most = ranks(heads_out, branches)
    tiles_out = ceil_div(most * steps, z_count)
    kv_core = KVH // CORES
    project = np.zeros((branches, heads_in), np.int32)
    for head, rank in rank_in.items():
        project[head // heads_in, head % heads_in] = rank * steps * CORES + key_head(head) % CORES
    fetch = np.zeros((z_count, CORES, kv_core, GROUP + 2, steps), np.int32)
    send = np.zeros((CORES, kv_core, GROUP, steps), np.int32)
    mix = np.zeros((z_count, CORES, branches, heads_out, steps), np.int32)
    for s in range(steps):
        for core in range(CORES):
            for j in range(kv_core):
                key = j * CORES + core
                heads = [key * GROUP + g for g in range(GROUP)] + [HEADS + key, HEADS + KVH + key]
                for n, head in enumerate(heads):
                    chip, tile = divmod(rank_in[head] * steps + s, tiles_in)
                    for z in range(z_count):
                        row = (chip ^ z) * branches + head // heads_in
                        fetch[z, core, j, n, s] = row * tiles_in + tile
                    if head < HEADS:
                        chip, tile = divmod(rank_out[head] * steps + s, tiles_out)
                        row = chip * branches + head // heads_out
                        send[core, j, n, s] = row * LANE + tile
        for head, rank in rank_out.items():
            chip, tile = divmod(rank * steps + s, tiles_out)
            for z in range(z_count):
                for core in range(CORES):
                    side = (key_head(head) % CORES) ^ core
                    row = side * z_count + (chip ^ z)
                    mix[z, core, head // heads_out, head % heads_out, s] = row * LANE + tile
    full = (z_count, CORES, branches)
    parts = [
        np.broadcast_to(project[None, None], full + project.shape[1:]),
        np.broadcast_to(fetch.reshape(z_count, CORES, 1, -1), full + (fetch[0, 0].size,)),
        np.broadcast_to(send.reshape(1, CORES, 1, -1), full + (send[0].size,)),
        mix.reshape(full + (-1,)),
    ]
    starts = np.cumsum([0] + [p.shape[-1] for p in parts]).tolist()
    return tiles_in, tiles_out, np.concatenate(parts, axis=-1), starts


def streamed(count, ahead, copies, work):
    for i in range(min(ahead, count)):
        for c in copies(i):
            c.start()

    def step(i, carry):
        for c in copies(i):
            c.wait()

        @pl.when(i + ahead < count)
        def _():
            for c in copies(i + ahead):
                c.start()

        work(i)
        return carry

    lax.fori_loop(0, count, step, 0)


def qkv_kernel(steps, heads_step, tiles, ids, table, lhs, w, out):
    columns = heads_step * HD
    branches = out.shape[2]
    for i in range(w.shape[1] // columns):
        acc = jnp.dot(
            lhs[...], w[:, i * columns : (i + 1) * columns], preferred_element_type=F32
        )
        for hh in range(heads_step):
            code = table[i * heads_step + hh]
            side = (code % CORES) ^ ids[1]
            for s in range(steps):
                index = code // CORES + s
                for k in range(branches):
                    row = (k * steps + s) * SUB
                    out[side, index // tiles, ids[2] ^ k, index % tiles] = acc[
                        row : row + SUB, hh * HD : (hh + 1) * HD
                    ]


def project_qkv(ids, table, lhs, w, steps, z_count, branches, tiles):
    heads = w.shape[1] // HD
    heads_step = max(n for n in range(1, 5) if heads % n == 0)
    shape = (CORES, z_count, branches, tiles, SUB, HD)
    return pl.pallas_call(
        functools.partial(qkv_kernel, steps, heads_step, tiles),
        in_specs=[IN_SMEM, IN_SMEM, IN_VMEM, IN_VMEM],
        out_shape=jax.ShapeDtypeStruct(shape, F32),
        compiler_params=params(24),
        cost_estimate=cost(lhs.shape[0], w.shape),
        name="qkv",
    )(ids, table, lhs, w)


def gate_up_kernel(unit, start, ids, lhs, w, out, buffer, sems):
    count = buffer.shape[0]
    part = buffer.shape[3]
    z_count = out.shape[1]

    def copies(i):
        at = pl.multiple_of(i * unit + start, LANE)
        return [
            pltpu.make_async_copy(w.at[g, :, pl.ds(at, part)], buffer.at[i, g], sems.at[i, g])
            for g in range(2)
        ]

    def work(i):
        side = (i % CORES) ^ ids[1]
        far = mirror((i // CORES) ^ ids[0], z_count)
        for g in range(2):
            product = jnp.dot(lhs[...], buffer[i, g], preferred_element_type=F32)
            out[side, far, g] = product.astype(BF16)

    streamed(count, 3, copies, work)


def project_gate_up(ids, lhs, w, unit, start, part, z_count):
    rows = lhs.shape[0]
    _, depth, columns = w.shape
    count = columns // unit
    shape = (CORES, z_count, 2, rows, part)
    return pl.pallas_call(
        functools.partial(gate_up_kernel, unit, start),
        in_specs=[IN_SMEM, IN_VMEM, IN_HBM],
        out_shape=jax.ShapeDtypeStruct(shape, BF16),
        scratch_shapes=[
            pltpu.VMEM((count, 2, depth, part), BF16),
            pltpu.SemaphoreType.DMA((count, 2)),
        ],
        compiler_params=params(32),
        cost_estimate=cost(rows, (depth, 2 * count * part)),
        name="gate_up",
    )(ids, lhs, w)


def mix_kernel(steps, base, ids, table, attended, w, first, second, lhs):
    unit = min(first.shape[3], 256)
    count = w.shape[1] // unit
    for j in range(lhs.shape[1] // HD):
        codes = [table[base + j * steps + s] for s in range(steps)]
        column = [
            attended[code // LANE, ids[2] ^ k, code % LANE].astype(F32)
            for k in range(first.shape[0])
            for code in codes
        ]
        lhs[:, j * HD : (j + 1) * HD] = jnp.concatenate(column, axis=0).astype(BF16)
    for i in range(count):
        acc = jnp.dot(lhs[...], w[:, i * unit : (i + 1) * unit], preferred_element_type=F32)
        out = first if i < count // 2 else second
        at = slice(i % (count // 2) * unit, (i % (count // 2) + 1) * unit)
        out[:, :, :, at] = acc.reshape(out.shape[:3] + (unit,)).astype(BF16)


def mix_heads(ids, table, base, attended, w, steps):
    branches = attended.shape[1]
    depth, columns = w.shape
    rows = branches * steps * SUB
    half = jax.ShapeDtypeStruct((branches, steps, SUB, columns // 2), BF16)
    return pl.pallas_call(
        functools.partial(mix_kernel, steps, base),
        in_specs=[IN_SMEM, IN_SMEM, IN_VMEM, IN_VMEM],
        out_shape=[half, half],
        scratch_shapes=[pltpu.VMEM((rows, depth), BF16)],
        compiler_params=params(24),
        cost_estimate=cost(rows, w.shape),
        name="mix",
    )(ids, table, attended, w)


def down_kernel(unit, start, table, *refs):
    *prior, activation, w, out, acc, buffer, sems = refs
    part = buffer.shape[1]
    acc[...] = prior[0][...] if prior else jnp.zeros_like(acc)

    def copies(i):
        at = pl.multiple_of(i * unit + start, LANE)
        return [pltpu.make_async_copy(w.at[pl.ds(at, part), :], buffer.at[i], sems.at[i])]

    def work(i):
        acc[...] += jnp.dot(activation[table[i]], buffer[i], preferred_element_type=F32)

    streamed(buffer.shape[0], min(6, buffer.shape[0]), copies, work)
    out[...] = acc[...].reshape(out.shape).astype(out.dtype)


def project_down(table, prior, activation, w, unit, start, shape):
    rows, part = activation.shape[1:]
    columns = w.shape[1]
    count = w.shape[0] // unit
    last = shape is not None
    result = (shape, BF16) if last else ((rows, columns), F32)
    return pl.pallas_call(
        functools.partial(down_kernel, unit, start),
        in_specs=[IN_SMEM] + [IN_VMEM] * (len(prior) + 1) + [IN_HBM],
        out_specs=IN_VMEM,
        out_shape=jax.ShapeDtypeStruct(*result),
        scratch_shapes=[
            pltpu.VMEM((rows, columns), F32),
            pltpu.VMEM((count, part, columns), BF16),
            pltpu.SemaphoreType.DMA((count,)),
        ],
        compiler_params=params(52),
        cost_estimate=cost(rows, (count * part, columns)),
        name="down",
    )(table, *prior, activation, w)


def prepare_kernel(steps, blocks_here, suffix_here, ids, parent, block_map, leaf, length, pos, bias):
    rows = leaf.shape[0]
    places = [ids[0] * CORES + (ids[1] ^ side) for side in range(CORES)]
    slots = [place * blocks_here + n for place in places for n in range(blocks_here)]
    sub = lax.broadcasted_iota(jnp.int32, (SUB, LANE), 0)
    base = jnp.zeros((SUB, LANE), jnp.int32)
    used = jnp.zeros((SUB, LANE), jnp.int32)
    owned = [jnp.zeros((SUB, LANE), jnp.int32) for _ in slots]
    for r in range(rows):
        current = leaf[r]
        depth = jnp.int32(0)
        hits = [jnp.int32(0)] * len(slots)
        for _ in range(parent.shape[0]):
            valid = current >= 0
            at = jnp.maximum(current, 0)
            found = jnp.where(valid, block_map[at], -1)
            hits = [h + (found == slot).astype(jnp.int32) for slot, h in zip(slots, hits)]
            depth = depth + valid.astype(jnp.int32)
            current = jnp.where(valid, parent[at], -1)
        base = jnp.where(sub == r, BLK * depth + length[r], base)
        used = jnp.where(sub == r, length[r], used)
        owned = [jnp.where(sub == r, h, o) for h, o in zip(hits, owned)]
    keys = SUB * suffix_here
    key_row = lax.broadcasted_iota(jnp.int32, (SUB, keys), 0)
    key = lax.broadcasted_iota(jnp.int32, (SUB, keys), 1)
    columns = [
        jnp.broadcast_to(jnp.where(o[:, :1] > 0, 0.0, FLOOR), (SUB, BLK)) for o in owned
    ]
    for place in places:
        ok = (key // suffix_here == key_row) & (
            place * suffix_here + key % suffix_here < used[:, :1]
        )
        columns.append(jnp.where(ok, 0.0, FLOOR))
    shared = jnp.concatenate(columns, axis=1)
    start = shared.shape[1]
    lane = lax.broadcasted_iota(jnp.int32, (SUB, LANE), 1)
    for s in range(steps):
        pos[s] = (base + s).astype(F32)
        row = slice(s * SUB, (s + 1) * SUB)
        bias[row, :start] = shared
        new_ok = (lane % SUB == sub) & (lane // SUB <= s) & (ids[0] == 0)
        bias[row, start : start + LANE] = jnp.where(new_ok, 0.0, FLOOR)


def prepare(ids, parent, block_map, leaf, length, steps, blocks_here, suffix_here):
    columns = CORES * (blocks_here * BLK + SUB * suffix_here) + LANE
    return pl.pallas_call(
        functools.partial(prepare_kernel, steps, blocks_here, suffix_here),
        in_specs=[IN_SMEM] * 5,
        out_specs=[IN_VMEM, IN_VMEM],
        out_shape=[
            jax.ShapeDtypeStruct((steps, SUB, LANE), F32),
            jax.ShapeDtypeStruct((steps * SUB, columns), F32),
        ],
        cost_estimate=pl.CostEstimate(flops=2**22, bytes_accessed=2**20, transcendentals=0),
        name="prepare",
    )(ids, parent, block_map, leaf, length)


def attend_kernel(
    fetch, send, table, qkv, cosine, sine, bias, tree, tree_two, suffix, suffix_two, out, new_kv, sums
):
    steps = cosine.shape[0]
    rows = steps * SUB
    tiles_out = out.shape[1] - 1
    kv_core = KVH // CORES
    lane = lax.broadcasted_iota(jnp.int32, (SUB, LANE), 1)
    sums[...] = jnp.zeros_like(sums)

    def turned(x, s):
        return x * cosine[s] + pltpu.roll(x, HD // 2, 1) * sine[s]

    for j in range(kv_core):

        def tile(n, s):
            return qkv[table[fetch + (j * (GROUP + 2) + n) * steps + s]].astype(F32)

        query = jnp.concatenate(
            [turned(tile(g, s), s) for g in range(GROUP) for s in range(steps)], axis=0
        ).astype(BF16)
        keys = [turned(tile(GROUP, s), s) for s in range(steps)]
        values = [tile(GROUP + 1, s) for s in range(steps)]
        at = slice(j * HD, (j + 1) * HD)
        for s in range(steps):
            new_kv[0, s, :, at] = keys[s].astype(BF16)
            new_kv[1, s, :, at] = values[s].astype(BF16)
        fill = [jnp.zeros((LANE - rows, HD), F32)]
        sources = [
            (kv[:, 0, :, at].reshape(-1, HD), kv[:, 1, :, at].reshape(-1, HD))
            for kv in (tree, tree_two, suffix, suffix_two)
        ]
        sources.append(
            (
                jnp.concatenate(keys + fill, axis=0).astype(BF16),
                jnp.concatenate(values + fill, axis=0).astype(BF16),
            )
        )
        scores = []
        start = 0
        highest = jnp.full((GROUP, rows, 1), LOWEST, F32)
        for key, _ in sources:
            count = key.shape[0]
            product = lax.dot_general(
                query, key, (((1,), (1,)), ((), ())), preferred_element_type=F32
            ) * (HD**-0.5)
            product = product.reshape(GROUP, rows, count) + bias[:, start : start + count][None]
            highest = jnp.maximum(highest, jnp.max(product, axis=-1, keepdims=True))
            scores.append(product)
            start += count
        total = jnp.zeros((GROUP, rows, 1), F32)
        acc = jnp.zeros((GROUP * rows, HD), F32)
        for product, (_, value) in zip(scores, sources):
            weight = jnp.exp(product - highest)
            total = total + jnp.sum(weight, axis=-1, keepdims=True)
            acc = acc + jnp.dot(
                weight.reshape(GROUP * rows, -1).astype(BF16), value, preferred_element_type=F32
            )
        some = total > 0
        safe = jnp.where(some, total, 1.0)
        result = acc.reshape(GROUP, rows, HD) / safe
        log_sum = jnp.where(some, highest + jnp.log(safe), LOWEST)
        for g in range(GROUP):
            for s in range(steps):
                code = table[send + (j * GROUP + g) * steps + s]
                place, t = code // LANE, code % LANE
                row = slice(s * SUB, (s + 1) * SUB)
                out[place, t] = result[g, row].astype(BF16)
                sums[place] = jnp.where(lane == t, log_sum[g, row], sums[place])

    for p in range(sums.shape[0]):
        out[p, tiles_out] = pack_sums(sums[p])


def pack_sums(value):
    lane = lax.broadcasted_iota(jnp.int32, (SUB, LANE), 1)
    high = value.astype(BF16).astype(F32)
    rest = value - high
    middle = rest.astype(BF16).astype(F32)
    low = rest - middle
    lows = jnp.where(lane < 64, pltpu.roll(middle, 32, 1), pltpu.roll(low, 64, 1))
    return jnp.where(lane < 32, high, lows).astype(BF16)


def attend(table, fetch, send, qkv, cosine, sine, bias, sources, devices, tiles):
    steps = cosine.shape[0]
    kv_core = KVH // CORES
    shape = (devices, tiles + 1, SUB, HD)
    return pl.pallas_call(
        functools.partial(attend_kernel, fetch, send),
        in_specs=[IN_SMEM] + [IN_VMEM] * 8,
        out_specs=[IN_VMEM, IN_VMEM],
        out_shape=[
            jax.ShapeDtypeStruct(shape, BF16),
            jax.ShapeDtypeStruct((2, steps, SUB, kv_core * HD), BF16),
        ],
        scratch_shapes=[pltpu.VMEM((devices, SUB, LANE), F32)],
        compiler_params=params(32),
        cost_estimate=pl.CostEstimate(
            flops=2**30, bytes_accessed=2 * sum(a.size for a in sources), transcendentals=2**21
        ),
        name="attend",
    )(table, qkv, cosine, sine, bias, *sources)


def cut_kernel(ids, *refs):
    *arrays, sems = refs
    sources, outs = arrays[: len(arrays) // 3], arrays[len(arrays) // 3 :]
    copies = []
    for n, source in enumerate(sources):
        for side in range(CORES):
            for j in range(KVH // CORES):
                head = j * CORES + (ids[1] ^ side)
                at = pl.ds(pl.multiple_of(head * HD, HD), HD)
                copies.append(
                    pltpu.make_async_copy(
                        source.at[:, :, :, at],
                        outs[n * CORES + side].at[:, :, :, pl.ds(j * HD, HD)],
                        sems.at[len(copies)],
                    )
                )
    for c in copies:
        c.start()
    for c in copies:
        c.wait()


def trade_heads(ids, *arrays):
    halves = [
        jax.ShapeDtypeStruct(a.shape[:-1] + (a.shape[-1] // CORES,), BF16)
        for a in arrays
        for _ in range(CORES)
    ]
    cut = pl.pallas_call(
        cut_kernel,
        in_specs=[IN_SMEM] + [IN_HBM] * len(arrays),
        out_specs=[IN_HBM] * len(halves),
        out_shape=halves,
        scratch_shapes=[pltpu.SemaphoreType.DMA((len(arrays) * KVH,))],
        compiler_params=params(4),
        cost_estimate=pl.CostEstimate(flops=0, bytes_accessed=2**23, transcendentals=0),
        name="cut",
    )(ids, *arrays)
    return [
        x if n % CORES == 0 else swap(x, "core", 1) for n, x in enumerate(cut)
    ]


def both_cores(own):
    other = swap(own, "core", 1)
    first = lax.axis_index("core") == 0
    even, odd = jnp.where(first, own, other), jnp.where(first, other, own)
    count = own.shape[-1] // HD
    spans = [slice(n * HD, (n + 1) * HD) for n in range(count)]
    return jnp.concatenate([x[..., at] for at in spans for x in (even, odd)], axis=-1)


def join_kernel(parts, out):
    prefix, branches, count = parts.shape[:3]
    tiles = count - 1
    for b in range(branches):
        logs = []
        for p in range(prefix):
            packed = parts[p, b, tiles].astype(F32)
            logs.append(packed + pltpu.roll(packed, LANE - 32, 1) + pltpu.roll(packed, LANE - 64, 1))
        highest = functools.reduce(jnp.maximum, logs)
        weights = [jnp.exp(x - highest) for x in logs]
        total = functools.reduce(jnp.add, weights)
        weights = [w / total for w in weights]
        for t in range(tiles):
            acc = jnp.zeros((SUB, HD), F32)
            for p in range(prefix):
                acc = acc + parts[p, b, t].astype(F32) * weights[p][:, t : t + 1]
            out[b, t] = acc.astype(BF16)


def join(parts):
    _, branches, count = parts.shape[:3]
    return pl.pallas_call(
        join_kernel,
        in_specs=[IN_VMEM],
        out_specs=IN_VMEM,
        out_shape=jax.ShapeDtypeStruct((branches, count - 1, SUB, HD), BF16),
        compiler_params=params(8),
        name="join",
    )(parts)


def body(
    hidden,
    attn_gain,
    ffn_gain,
    w_qkv,
    w_out,
    w_gate_up,
    w_down,
    tree_kv,
    suffix_kv,
    parent,
    block_map,
    leaf,
    suffix_len,
):
    steps, rows, width_dev = hidden.shape
    z_count = lax.axis_size("z")
    branches = lax.axis_size("branch")
    prefix = z_count * CORES
    width = width_dev * prefix
    near = bits(z_count)
    across = bits(branches)
    places = place_table()
    ids = jnp.stack([lax.axis_index(a) for a in AXES]).astype(jnp.int32)

    tiles_in, tiles_out, table, (_, fetch, send, mix, _) = head_tables(steps, z_count, branches)
    table = jnp.asarray(table)[tuple(lax.axis_index(a) for a in AXES)]
    pos, bias = prepare(
        ids, parent, block_map, leaf, suffix_len, steps, tree_kv.shape[0], suffix_kv.shape[2]
    )
    half = HD // 2
    frequency = ROPE_BASE ** (-(jnp.arange(half, dtype=F32) * 2.0 / HD))
    angles = pos[..., :1] * frequency
    cos, sin = jnp.cos(angles), jnp.sin(angles)
    cosine = jnp.concatenate([cos, cos], axis=-1)
    sine = jnp.concatenate([-sin, sin], axis=-1)

    every_row = gather(hidden, "branch")
    every_row, tree_kv, suffix_kv = lax.optimization_barrier((every_row, tree_kv, suffix_kv))
    lhs = norm_rows(every_row, attn_gain, width)
    sources = trade_heads(ids, tree_kv, suffix_kv)
    lhs, table, sources, cosine, sine, bias = lax.optimization_barrier(
        (lhs, table, sources, cosine, sine, bias)
    )
    part_sums = project_qkv(ids, table, lhs, w_qkv, steps, z_count, branches, tiles_in)
    chip_sums = part_sums[0] + swap(part_sums[1], "core", 1)
    plane = z_count * branches
    received = exchange(chip_sums.reshape(plane, tiles_in, SUB, HD), ("z", "branch"))
    summed = jnp.sum(received.reshape(z_count, branches, tiles_in, SUB, HD), axis=0).astype(BF16)
    qkv = gather(summed, "z").reshape(-1, SUB, HD)

    softmax_parts, new_kv = attend(
        table, fetch, send, qkv, cosine, sine, bias, sources, plane, tiles_out
    )
    received = exchange(softmax_parts, ("z", "branch"))
    attended = join(received.reshape(z_count, branches, tiles_out + 1, SUB, HD))
    attended = gather_rounds(gather(attended, "z"), "core", [1])
    attended = attended.reshape((prefix,) + attended.shape[2:])
    new_kv = both_cores(new_kv).transpose(2, 0, 1, 3)

    mixed = sum_branches(*mix_heads(ids, table, mix, attended, w_out, steps))
    residual = (every_row.astype(F32) + mixed).astype(BF16)
    lhs = norm_rows(residual, ffn_gain, width)

    unit = ceil_div(w_gate_up.shape[2] // LANE, prefix) * LANE
    first = ceil_div(unit // LANE, 2) * LANE
    spans = [(at, size) for at, size in ((0, first), (first, unit - first)) if size]
    down = []
    for start, part in spans:
        part_sums = project_gate_up(ids, lhs, w_gate_up, unit, start, part, z_count)
        chip_sums = add(part_sums[0], swap(part_sums[1], "core", 1))
        lhs, chip_sums = lax.optimization_barrier((lhs, chip_sums))
        gate, up = add_round(chip_sums, "z", near)
        activation = gather_prefix((jax.nn.silu(gate) * up).astype(BF16))
        shape = (branches, steps, rows, width_dev) if start == spans[-1][0] else None
        down = [project_down(places, down, activation, w_down, unit, start, shape)]
    result = (residual[0].astype(F32) + own_sum(down[0])).astype(BF16)
    return (result, new_kv)


def solution(mesh):
    prefix, branches = mesh.shape["prefix"], mesh.shape["branch"]
    split = Mesh(mesh.devices.reshape(prefix // CORES, CORES, branches), AXES)
    along = ("z", "core")
    placed = (
        P(None, "branch", along),
        P(along),
        P(along),
        P(along, "branch"),
        P("branch", along),
        P(None, along, "branch"),
        P("branch", along),
        P(along, None, None, None),
        P("branch", None, along, None),
        P(),
        P(),
        P("branch"),
        P("branch"),
    )
    return jax.shard_map(
        body,
        mesh=split,
        in_specs=placed,
        out_specs=(P(None, "branch", along), P("branch", None, None, None)),
        check_vma=False,
    )
```

```python
import functools

import jax
import jax.numpy as jnp
import numpy as np
from jax import lax
from jax.experimental import pallas as pl
from jax.experimental.pallas import tpu as pltpu
from jax.sharding import Mesh
from jax.sharding import PartitionSpec as P

HEADS = 64
KVH = 8
HD = 128
GROUP = HEADS // KVH
BLK = 512
CORES = 2
SUB = 8
LANE = 128

EPS = 1e-05
ROPE_BASE = 500000.0
FLOOR = -1e30
LOWEST = -1e29
F32 = jnp.float32
BF16 = jnp.bfloat16
AXES = ("z", "core", "branch")


def ceil_div(a, b):
    return -(-a // b)


def whole(shape):
    return pl.BlockSpec(shape, lambda *_: (0,) * len(shape))


def cost(rows, w):
    return pl.CostEstimate(
        flops=2 * rows * w[0] * w[1], bytes_accessed=2 * w[0] * w[1], transcendentals=0
    )


def exchange(x, axes):
    return lax.all_to_all(x, axes, split_axis=0, concat_axis=0, tiled=True)


def params(mib):
    return pltpu.CompilerParams(vmem_limit_bytes=mib * 2**20)


IN_HBM = pl.BlockSpec(memory_space=pltpu.HBM)
IN_VMEM = pl.BlockSpec(memory_space=pltpu.VMEM)
IN_SMEM = pl.BlockSpec(memory_space=pltpu.SMEM)


def bits(n):
    return [1 << i for i in range(n.bit_length() - 1)]


def mirror(q, n):
    out = 0
    top = n.bit_length() - 2
    for i in range(top + 1):
        out = out + (((q >> i) & 1) << (top - i))
    return out


def swap(x, axis, bit):
    return lax.ppermute(x, axis, [(i, i ^ bit) for i in range(lax.axis_size(axis))])


def reduce_rounds(x, axis, order):
    for bit in order:
        half = x.shape[0] // 2
        x = x[:half] + swap(x[half:], axis, bit)
    return x[0]


def gather_rounds(x, axis, order):
    x = x[None]
    for bit in order:
        x = jnp.concatenate([x, swap(x, axis, bit)], axis=0)
    return x


def gather(x, axis):
    n = lax.axis_size(axis)
    if n > 4:
        return gather_rounds(x, axis, bits(n))
    return jnp.stack([x] + [swap(x, axis, k) for k in range(1, n)])


def total_along(x, axis):
    n = lax.axis_size(axis)
    if n > 4:
        for bit in bits(n):
            x = x + swap(x, axis, bit)
        return x
    return functools.reduce(jnp.add, [x] + [swap(x, axis, k) for k in range(1, n)])


def sum_chips(x):
    n = x.shape[0]
    if n > 4:
        return reduce_rounds(x, "z", bits(n)[::-1])
    return functools.reduce(jnp.add, [x[0]] + [swap(x[k], "z", k) for k in range(1, n)])


def add_round(x, axis, order):
    for bit in order:
        half = x.shape[0] // 2
        kept = x[:half].astype(F32)
        kept = kept + swap(x[half:], axis, bit).astype(F32)
        x = kept.astype(BF16)
    return kept[0]


def add(a, b):
    return (a.astype(F32) + b.astype(F32)).astype(BF16)


def as_tile(x):
    return jnp.pad(x, ((0, -x.shape[0] % SUB), (0, LANE - x.shape[1])))


def normed(x, squares, gain, width):
    scale = lax.rsqrt(squares / width + EPS)
    return (x * scale[..., None] * gain).astype(BF16)


def norm_rows(x, gain, width):
    value = x.astype(F32)
    squares = jnp.sum(value * value, axis=3)
    total = as_tile(squares.reshape(-1, squares.shape[-1]))
    total = total + swap(total, "core", 1)
    total = total_along(total, "z")
    total = total[: squares.shape[0] * squares.shape[1], : squares.shape[2]].reshape(squares.shape)
    return normed(value, total, gain, width).reshape(-1, x.shape[3])


def sum_round(x, bit):
    other = swap(x, "branch", bit).astype(F32)
    shape = other.shape
    other = jnp.flip(other.reshape((shape[0] // (2 * bit), 2, bit) + shape[1:]), axis=1)
    return x.astype(F32) + other.reshape(shape)


def sum_branches(first, second):
    order = bits(lax.axis_size("branch"))
    for one, two in zip(order, order[::-1]):
        first, second = sum_round(first.astype(BF16), one), sum_round(second.astype(BF16), two)
    return jnp.concatenate([first, second], axis=-1)


def own_sum(x):
    n = x.shape[0]
    if n > 4:
        return add_round(x, "branch", bits(n)[::-1])
    arrived = [swap(x[k], "branch", k) for k in range(1, n)]
    return functools.reduce(jnp.add, [a.astype(F32) for a in [x[0]] + arrived])


def gather_prefix(x, direct):
    x = gather(x, "z") if direct else gather_rounds(x, "z", bits(lax.axis_size("z"))[::-1])
    x = gather_rounds(x, "core", [1])
    return x.reshape((-1,) + x.shape[2:])


def place_table(direct):
    z_count = lax.axis_size("z")
    owner = jnp.arange(z_count * CORES, dtype=jnp.int32)
    far = (owner // CORES) ^ lax.axis_index("z")
    far = far if direct else mirror(far, z_count)
    return (((owner % CORES) ^ lax.axis_index("core")) * z_count + far).astype(jnp.int32)


def key_head(head):
    return head // GROUP if head < HEADS else (head - HEADS) % KVH


def ranks(heads_each, branches):
    rank, most = {}, 0
    for b in range(branches):
        count = [0] * CORES
        for head in range(b * heads_each, (b + 1) * heads_each):
            core = key_head(head) % CORES
            rank[head] = count[core]
            count[core] += 1
        most = max(most, *count)
    return rank, most


def head_tables(steps, z_count, branches):
    heads_in = (HEADS + 2 * KVH) // branches
    heads_out = HEADS // branches
    rank_in, most = ranks(heads_in, branches)
    tiles_in = ceil_div(most * steps, z_count)
    rank_out, most = ranks(heads_out, branches)
    tiles_out = ceil_div(most * steps, z_count)
    kv_core = KVH // CORES
    project = np.zeros((branches, heads_in), np.int32)
    for head, rank in rank_in.items():
        project[head // heads_in, head % heads_in] = rank * steps * CORES + key_head(head) % CORES
    fetch = np.zeros((z_count, CORES, branches, kv_core, GROUP + 2, steps), np.int32)
    send = np.zeros((CORES, kv_core, GROUP, steps), np.int32)
    mix = np.zeros((z_count, CORES, branches, heads_out, steps), np.int32)
    for s in range(steps):
        for core in range(CORES):
            for j in range(kv_core):
                key = j * CORES + core
                heads = [key * GROUP + g for g in range(GROUP)] + [HEADS + key, HEADS + KVH + key]
                for n, head in enumerate(heads):
                    chip, tile = divmod(rank_in[head] * steps + s, tiles_in)
                    for z in range(z_count):
                        for b in range(branches):
                            row = (chip ^ z) * branches + (head // heads_in ^ b)
                            fetch[z, core, b, j, n, s] = row * tiles_in + tile
                    if head < HEADS:
                        chip, tile = divmod(rank_out[head] * steps + s, tiles_out)
                        row = chip * branches + head // heads_out
                        send[core, j, n, s] = row * LANE + tile
        for head, rank in rank_out.items():
            chip, tile = divmod(rank * steps + s, tiles_out)
            for z in range(z_count):
                for core in range(CORES):
                    side = (key_head(head) % CORES) ^ core
                    row = side * z_count + (chip ^ z)
                    mix[z, core, head // heads_out, head % heads_out, s] = row * LANE + tile
    full = (z_count, CORES, branches)
    parts = [
        np.broadcast_to(project[None, None], full + project.shape[1:]),
        fetch.reshape(full + (-1,)),
        np.broadcast_to(send.reshape(1, CORES, 1, -1), full + (send[0].size,)),
        mix.reshape(full + (-1,)),
    ]
    starts = np.cumsum([0] + [p.shape[-1] for p in parts]).tolist()
    return tiles_in, tiles_out, np.concatenate(parts, axis=-1), starts


def streamed(count, ahead, copies, work):
    for i in range(min(ahead, count)):
        for c in copies(i):
            c.start()

    def step(i, carry):
        for c in copies(i):
            c.wait()

        @pl.when(i + ahead < count)
        def _():
            for c in copies(i + ahead):
                c.start()

        work(i)
        return carry

    lax.fori_loop(0, count, step, 0)


def qkv_kernel(steps, heads_step, tiles, ids, table, lhs, w, out):
    columns = heads_step * HD
    branches = out.shape[2]
    for i in range(w.shape[1] // columns):
        acc = jnp.dot(
            lhs[...], w[:, i * columns : (i + 1) * columns], preferred_element_type=F32
        )
        for hh in range(heads_step):
            code = table[i * heads_step + hh]
            side = (code % CORES) ^ ids[1]
            for s in range(steps):
                index = code // CORES + s
                for k in range(branches):
                    row = (k * steps + s) * SUB
                    out[side, (index // tiles) ^ ids[0], k, index % tiles] = acc[
                        row : row + SUB, hh * HD : (hh + 1) * HD
                    ]


def project_qkv(ids, table, lhs, w, steps, z_count, branches, tiles):
    heads = w.shape[1] // HD
    heads_step = max(n for n in range(1, 5) if heads % n == 0)
    shape = (CORES, z_count, branches, tiles, SUB, HD)
    return pl.pallas_call(
        functools.partial(qkv_kernel, steps, heads_step, tiles),
        in_specs=[IN_SMEM, IN_SMEM, IN_VMEM, IN_VMEM],
        out_shape=jax.ShapeDtypeStruct(shape, F32),
        compiler_params=params(24),
        cost_estimate=cost(lhs.shape[0], w.shape),
        name="qkv",
    )(ids, table, lhs, w)


def gate_up_kernel(unit, start, ids, lhs, w, out, buffer, sems):
    count = buffer.shape[0]
    part = buffer.shape[3]
    z_count = out.shape[1]

    def copies(i):
        at = pl.multiple_of(i * unit + start, LANE)
        return [
            pltpu.make_async_copy(w.at[g, :, pl.ds(at, part)], buffer.at[i, g], sems.at[i, g])
            for g in range(2)
        ]

    def work(i):
        side = (i % CORES) ^ ids[1]
        far = mirror((i // CORES) ^ ids[0], z_count)
        for g in range(2):
            product = jnp.dot(lhs[...], buffer[i, g], preferred_element_type=F32)
            out[side, far, g] = product.astype(BF16)

    streamed(count, 3, copies, work)


def project_gate_up(ids, lhs, w, unit, start, part, z_count):
    rows = lhs.shape[0]
    _, depth, columns = w.shape
    count = columns // unit
    shape = (CORES, z_count, 2, rows, part)
    return pl.pallas_call(
        functools.partial(gate_up_kernel, unit, start),
        in_specs=[IN_SMEM, IN_VMEM, IN_HBM],
        out_shape=jax.ShapeDtypeStruct(shape, BF16),
        scratch_shapes=[
            pltpu.VMEM((count, 2, depth, part), BF16),
            pltpu.SemaphoreType.DMA((count, 2)),
        ],
        compiler_params=params(32),
        cost_estimate=cost(rows, (depth, 2 * count * part)),
        name="gate_up",
    )(ids, lhs, w)


def mix_kernel(steps, base, ids, table, attended, w, first, second, lhs):
    unit = min(first.shape[3], 256)
    count = w.shape[1] // unit
    for j in range(lhs.shape[1] // HD):
        codes = [table[base + j * steps + s] for s in range(steps)]
        column = [
            attended[code // LANE, ids[2] ^ k, code % LANE].astype(F32)
            for k in range(first.shape[0])
            for code in codes
        ]
        lhs[:, j * HD : (j + 1) * HD] = jnp.concatenate(column, axis=0).astype(BF16)
    for i in range(count):
        acc = jnp.dot(lhs[...], w[:, i * unit : (i + 1) * unit], preferred_element_type=F32)
        out = first if i < count // 2 else second
        at = slice(i % (count // 2) * unit, (i % (count // 2) + 1) * unit)
        out[:, :, :, at] = acc.reshape(out.shape[:3] + (unit,)).astype(BF16)


def mix_heads(ids, table, base, attended, w, steps):
    branches = attended.shape[1]
    depth, columns = w.shape
    rows = branches * steps * SUB
    half = jax.ShapeDtypeStruct((branches, steps, SUB, columns // 2), BF16)
    return pl.pallas_call(
        functools.partial(mix_kernel, steps, base),
        in_specs=[IN_SMEM, IN_SMEM, IN_VMEM, IN_VMEM],
        out_shape=[half, half],
        scratch_shapes=[pltpu.VMEM((rows, depth), BF16)],
        compiler_params=params(24),
        cost_estimate=cost(rows, w.shape),
        name="mix",
    )(ids, table, attended, w)


def down_kernel(unit, start, table, *refs):
    *prior, activation, w, out, acc, buffer, sems = refs
    part = buffer.shape[1]
    acc[...] = prior[0][...] if prior else jnp.zeros_like(acc)

    def copies(i):
        at = pl.multiple_of(i * unit + start, LANE)
        return [pltpu.make_async_copy(w.at[pl.ds(at, part), :], buffer.at[i], sems.at[i])]

    def work(i):
        acc[...] += jnp.dot(activation[table[i]], buffer[i], preferred_element_type=F32)

    streamed(buffer.shape[0], min(6, buffer.shape[0]), copies, work)
    out[...] = acc[...].reshape(out.shape).astype(out.dtype)


def project_down(table, prior, activation, w, unit, start, shape):
    rows, part = activation.shape[1:]
    columns = w.shape[1]
    count = w.shape[0] // unit
    last = shape is not None
    result = (shape, BF16) if last else ((rows, columns), F32)
    return pl.pallas_call(
        functools.partial(down_kernel, unit, start),
        in_specs=[IN_SMEM] + [IN_VMEM] * (len(prior) + 1) + [IN_HBM],
        out_specs=IN_VMEM,
        out_shape=jax.ShapeDtypeStruct(*result),
        scratch_shapes=[
            pltpu.VMEM((rows, columns), F32),
            pltpu.VMEM((count, part, columns), BF16),
            pltpu.SemaphoreType.DMA((count,)),
        ],
        compiler_params=params(52),
        cost_estimate=cost(rows, (count * part, columns)),
        name="down",
    )(table, *prior, activation, w)


def prepare_kernel(steps, blocks_here, suffix_here, ids, parent, block_map, leaf, length, pos, bias):
    rows = leaf.shape[0]
    places = [ids[0] * CORES + (ids[1] ^ side) for side in range(CORES)]
    slots = [place * blocks_here + n for place in places for n in range(blocks_here)]
    sub = lax.broadcasted_iota(jnp.int32, (SUB, LANE), 0)
    base = jnp.zeros((SUB, LANE), jnp.int32)
    used = jnp.zeros((SUB, LANE), jnp.int32)
    owned = [jnp.zeros((SUB, LANE), jnp.int32) for _ in slots]
    for r in range(rows):
        current = leaf[r]
        depth = jnp.int32(0)
        hits = [jnp.int32(0)] * len(slots)
        for _ in range(parent.shape[0]):
            valid = current >= 0
            at = jnp.maximum(current, 0)
            found = jnp.where(valid, block_map[at], -1)
            hits = [h + (found == slot).astype(jnp.int32) for slot, h in zip(slots, hits)]
            depth = depth + valid.astype(jnp.int32)
            current = jnp.where(valid, parent[at], -1)
        base = jnp.where(sub == r, BLK * depth + length[r], base)
        used = jnp.where(sub == r, length[r], used)
        owned = [jnp.where(sub == r, h, o) for h, o in zip(hits, owned)]
    keys = SUB * suffix_here
    key_row = lax.broadcasted_iota(jnp.int32, (SUB, keys), 0)
    key = lax.broadcasted_iota(jnp.int32, (SUB, keys), 1)
    columns = [
        jnp.broadcast_to(jnp.where(o[:, :1] > 0, 0.0, FLOOR), (SUB, BLK)) for o in owned
    ]
    for place in places:
        ok = (key // suffix_here == key_row) & (
            place * suffix_here + key % suffix_here < used[:, :1]
        )
        columns.append(jnp.where(ok, 0.0, FLOOR))
    shared = jnp.concatenate(columns, axis=1)
    start = shared.shape[1]
    lane = lax.broadcasted_iota(jnp.int32, (SUB, LANE), 1)
    for s in range(steps):
        pos[s] = (base + s).astype(F32)
        row = slice(s * SUB, (s + 1) * SUB)
        bias[row, :start] = shared
        new_ok = (lane % SUB == sub) & (lane // SUB <= s) & (ids[0] == 0)
        bias[row, start : start + LANE] = jnp.where(new_ok, 0.0, FLOOR)


def prepare(ids, parent, block_map, leaf, length, steps, blocks_here, suffix_here):
    columns = CORES * (blocks_here * BLK + SUB * suffix_here) + LANE
    return pl.pallas_call(
        functools.partial(prepare_kernel, steps, blocks_here, suffix_here),
        in_specs=[IN_SMEM] * 5,
        out_specs=[IN_VMEM, IN_VMEM],
        out_shape=[
            jax.ShapeDtypeStruct((steps, SUB, LANE), F32),
            jax.ShapeDtypeStruct((steps * SUB, columns), F32),
        ],
        cost_estimate=pl.CostEstimate(flops=2**22, bytes_accessed=2**20, transcendentals=0),
        name="prepare",
    )(ids, parent, block_map, leaf, length)


def attend_kernel(
    fetch, send, table, qkv, cosine, sine, bias, tree, tree_two, suffix, suffix_two, out, new_kv, sums
):
    steps = cosine.shape[0]
    rows = steps * SUB
    tiles_out = out.shape[1] - 1
    kv_core = KVH // CORES
    lane = lax.broadcasted_iota(jnp.int32, (SUB, LANE), 1)
    sums[...] = jnp.zeros_like(sums)

    def turned(x, s):
        return x * cosine[s] + pltpu.roll(x, HD // 2, 1) * sine[s]

    for j in range(kv_core):

        def tile(n, s):
            return qkv[table[fetch + (j * (GROUP + 2) + n) * steps + s]].astype(F32)

        query = jnp.concatenate(
            [turned(tile(g, s), s) for g in range(GROUP) for s in range(steps)], axis=0
        ).astype(BF16)
        keys = [turned(tile(GROUP, s), s) for s in range(steps)]
        values = [tile(GROUP + 1, s) for s in range(steps)]
        at = slice(j * HD, (j + 1) * HD)
        for s in range(steps):
            new_kv[0, s, :, at] = keys[s].astype(BF16)
            new_kv[1, s, :, at] = values[s].astype(BF16)
        fill = [jnp.zeros((LANE - rows, HD), F32)]
        sources = [
            (kv[:, 0, :, at].reshape(-1, HD), kv[:, 1, :, at].reshape(-1, HD))
            for kv in (tree, tree_two, suffix, suffix_two)
        ]
        sources.append(
            (
                jnp.concatenate(keys + fill, axis=0).astype(BF16),
                jnp.concatenate(values + fill, axis=0).astype(BF16),
            )
        )
        scores = []
        start = 0
        highest = jnp.full((GROUP, rows, 1), LOWEST, F32)
        for key, _ in sources:
            count = key.shape[0]
            product = lax.dot_general(
                query, key, (((1,), (1,)), ((), ())), preferred_element_type=F32
            ) * (HD**-0.5)
            product = product.reshape(GROUP, rows, count) + bias[:, start : start + count][None]
            highest = jnp.maximum(highest, jnp.max(product, axis=-1, keepdims=True))
            scores.append(product)
            start += count
        total = jnp.zeros((GROUP, rows, 1), F32)
        acc = jnp.zeros((GROUP * rows, HD), F32)
        for product, (_, value) in zip(scores, sources):
            weight = jnp.exp(product - highest)
            total = total + jnp.sum(weight, axis=-1, keepdims=True)
            acc = acc + jnp.dot(
                weight.reshape(GROUP * rows, -1).astype(BF16), value, preferred_element_type=F32
            )
        some = total > 0
        safe = jnp.where(some, total, 1.0)
        result = acc.reshape(GROUP, rows, HD) / safe
        log_sum = jnp.where(some, highest + jnp.log(safe), LOWEST)
        for g in range(GROUP):
            for s in range(steps):
                code = table[send + (j * GROUP + g) * steps + s]
                place, t = code // LANE, code % LANE
                row = slice(s * SUB, (s + 1) * SUB)
                out[place, t] = result[g, row].astype(BF16)
                sums[place] = jnp.where(lane == t, log_sum[g, row], sums[place])

    for p in range(sums.shape[0]):
        out[p, tiles_out] = pack_sums(sums[p])


def pack_sums(value):
    lane = lax.broadcasted_iota(jnp.int32, (SUB, LANE), 1)
    high = value.astype(BF16).astype(F32)
    rest = value - high
    middle = rest.astype(BF16).astype(F32)
    low = rest - middle
    lows = jnp.where(lane < 64, pltpu.roll(middle, 32, 1), pltpu.roll(low, 64, 1))
    return jnp.where(lane < 32, high, lows).astype(BF16)


def attend(table, fetch, send, qkv, cosine, sine, bias, sources, devices, tiles):
    steps = cosine.shape[0]
    kv_core = KVH // CORES
    shape = (devices, tiles + 1, SUB, HD)
    return pl.pallas_call(
        functools.partial(attend_kernel, fetch, send),
        in_specs=[IN_SMEM] + [IN_VMEM] * 8,
        out_specs=[IN_VMEM, IN_VMEM],
        out_shape=[
            jax.ShapeDtypeStruct(shape, BF16),
            jax.ShapeDtypeStruct((2, steps, SUB, kv_core * HD), BF16),
        ],
        scratch_shapes=[pltpu.VMEM((devices, SUB, LANE), F32)],
        compiler_params=params(32),
        cost_estimate=pl.CostEstimate(
            flops=2**30, bytes_accessed=2 * sum(a.size for a in sources), transcendentals=2**21
        ),
        name="attend",
    )(table, qkv, cosine, sine, bias, *sources)


def cut_kernel(ids, *refs):
    *arrays, sems = refs
    sources, outs = arrays[: len(arrays) // 3], arrays[len(arrays) // 3 :]
    copies = []
    for n, source in enumerate(sources):
        for side in range(CORES):
            for j in range(KVH // CORES):
                head = j * CORES + (ids[1] ^ side)
                at = pl.ds(pl.multiple_of(head * HD, HD), HD)
                copies.append(
                    pltpu.make_async_copy(
                        source.at[:, :, :, at],
                        outs[n * CORES + side].at[:, :, :, pl.ds(j * HD, HD)],
                        sems.at[len(copies)],
                    )
                )
    for c in copies:
        c.start()
    for c in copies:
        c.wait()


def trade_heads(ids, *arrays):
    halves = [
        jax.ShapeDtypeStruct(a.shape[:-1] + (a.shape[-1] // CORES,), BF16)
        for a in arrays
        for _ in range(CORES)
    ]
    cut = pl.pallas_call(
        cut_kernel,
        in_specs=[IN_SMEM] + [IN_HBM] * len(arrays),
        out_specs=[IN_HBM] * len(halves),
        out_shape=halves,
        scratch_shapes=[pltpu.SemaphoreType.DMA((len(arrays) * KVH,))],
        compiler_params=params(4),
        cost_estimate=pl.CostEstimate(flops=0, bytes_accessed=2**23, transcendentals=0),
        name="cut",
    )(ids, *arrays)
    return [
        x if n % CORES == 0 else swap(x, "core", 1) for n, x in enumerate(cut)
    ]


def both_cores(own):
    other = swap(own, "core", 1)
    first = lax.axis_index("core") == 0
    even, odd = jnp.where(first, own, other), jnp.where(first, other, own)
    count = own.shape[-1] // HD
    spans = [slice(n * HD, (n + 1) * HD) for n in range(count)]
    return jnp.concatenate([x[..., at] for at in spans for x in (even, odd)], axis=-1)


def join_kernel(parts, out):
    prefix, branches, count = parts.shape[:3]
    tiles = count - 1
    for b in range(branches):
        logs = []
        for p in range(prefix):
            packed = parts[p, b, tiles].astype(F32)
            logs.append(packed + pltpu.roll(packed, LANE - 32, 1) + pltpu.roll(packed, LANE - 64, 1))
        highest = functools.reduce(jnp.maximum, logs)
        weights = [jnp.exp(x - highest) for x in logs]
        total = functools.reduce(jnp.add, weights)
        weights = [w / total for w in weights]
        for t in range(tiles):
            acc = jnp.zeros((SUB, HD), F32)
            for p in range(prefix):
                acc = acc + parts[p, b, t].astype(F32) * weights[p][:, t : t + 1]
            out[b, t] = acc.astype(BF16)


def join(parts):
    _, branches, count = parts.shape[:3]
    return pl.pallas_call(
        join_kernel,
        in_specs=[IN_VMEM],
        out_specs=IN_VMEM,
        out_shape=jax.ShapeDtypeStruct((branches, count - 1, SUB, HD), BF16),
        compiler_params=params(8),
        name="join",
    )(parts)


def body(
    hidden,
    attn_gain,
    ffn_gain,
    w_qkv,
    w_out,
    w_gate_up,
    w_down,
    tree_kv,
    suffix_kv,
    parent,
    block_map,
    leaf,
    suffix_len,
):
    steps, rows, width_dev = hidden.shape
    z_count = lax.axis_size("z")
    branches = lax.axis_size("branch")
    prefix = z_count * CORES
    width = width_dev * prefix
    near = bits(z_count)
    across = bits(branches)
    ids = jnp.stack([lax.axis_index(a) for a in AXES]).astype(jnp.int32)

    tiles_in, tiles_out, table, (_, fetch, send, mix, _) = head_tables(steps, z_count, branches)
    table = jnp.asarray(table)[tuple(lax.axis_index(a) for a in AXES)]
    pos, bias = prepare(
        ids, parent, block_map, leaf, suffix_len, steps, tree_kv.shape[0], suffix_kv.shape[2]
    )
    half = HD // 2
    frequency = ROPE_BASE ** (-(jnp.arange(half, dtype=F32) * 2.0 / HD))
    angles = pos[..., :1] * frequency
    cos, sin = jnp.cos(angles), jnp.sin(angles)
    cosine = jnp.concatenate([cos, cos], axis=-1)
    sine = jnp.concatenate([-sin, sin], axis=-1)

    every_row = gather(hidden, "branch")
    every_row, tree_kv, suffix_kv = lax.optimization_barrier((every_row, tree_kv, suffix_kv))
    lhs = norm_rows(every_row, attn_gain, width)
    sources = trade_heads(ids, tree_kv, suffix_kv)
    lhs, table, sources, cosine, sine, bias = lax.optimization_barrier(
        (lhs, table, sources, cosine, sine, bias)
    )
    part_sums = project_qkv(ids, table, lhs, w_qkv, steps, z_count, branches, tiles_in)
    chip_sums = part_sums[0] + swap(part_sums[1], "core", 1)
    plane = z_count * branches
    summed = sum_chips(chip_sums).astype(BF16)
    summed = jnp.stack([summed[0]] + [swap(summed[k], "branch", k) for k in range(1, branches)])
    qkv = gather(summed, "z").reshape(-1, SUB, HD)

    softmax_parts, new_kv = attend(
        table, fetch, send, qkv, cosine, sine, bias, sources, plane, tiles_out
    )
    received = exchange(softmax_parts, ("z", "branch"))
    attended = join(received.reshape(z_count, branches, tiles_out + 1, SUB, HD))
    attended = gather_prefix(attended, True)
    new_kv = both_cores(new_kv).transpose(2, 0, 1, 3)

    mixed = sum_branches(*mix_heads(ids, table, mix, attended, w_out, steps))
    residual = (every_row.astype(F32) + mixed).astype(BF16)
    lhs = norm_rows(residual, ffn_gain, width)

    unit = ceil_div(w_gate_up.shape[2] // LANE, prefix) * LANE
    first = ceil_div(unit // LANE, 2) * LANE
    spans = [(at, size) for at, size in ((0, first), (first, unit - first)) if size]
    down = []
    for start, part in spans:
        part_sums = project_gate_up(ids, lhs, w_gate_up, unit, start, part, z_count)
        chip_sums = add(part_sums[0], swap(part_sums[1], "core", 1))
        lhs, chip_sums = lax.optimization_barrier((lhs, chip_sums))
        gate, up = add_round(chip_sums, "z", near)
        last = start == spans[-1][0]
        activation = gather_prefix((jax.nn.silu(gate) * up).astype(BF16), last)
        shape = (branches, steps, rows, width_dev) if last else None
        down = [project_down(place_table(last), down, activation, w_down, unit, start, shape)]
    result = (residual[0].astype(F32) + own_sum(down[0])).astype(BF16)
    return (result, new_kv)


def solution(mesh):
    prefix, branches = mesh.shape["prefix"], mesh.shape["branch"]
    split = Mesh(mesh.devices.reshape(prefix // CORES, CORES, branches), AXES)
    along = ("z", "core")
    placed = (
        P(None, "branch", along),
        P(along),
        P(along),
        P(along, "branch"),
        P("branch", along),
        P(None, along, "branch"),
        P("branch", along),
        P(along, None, None, None),
        P("branch", None, along, None),
        P(),
        P(),
        P("branch"),
        P("branch"),
    )
    return jax.shard_map(
        body,
        mesh=split,
        in_specs=placed,
        out_specs=(P(None, "branch", along), P("branch", None, None, None)),
        check_vma=False,
    )
```
